256 devices in a mesh: dp: 8 (over y, core), anchor: 16 (over z, x_hi), aug: 2 (over x_lo).
Axes of the slice: x: 4 (x_hi: 2, x_lo: 2; x = x_hi * 2 + x_lo), y: 4, z: 8, core: 2. Of those that a mesh axis runs over, the one named last changes fastest.
Arguments:
- anchor_hidden: bfloat16 [8, 512, 4608], P('dp', ('anchor', 'aug')), may hold values from -6 to 6
- aug_hidden: bfloat16 [8, 512, 2304], P('dp', ('anchor', 'aug')), may hold values from -6 to 6
- out_grad: bfloat16 [8, 512, 4608], P('dp', ('anchor', 'aug')), may hold values from -6 to 6
- w_query: bfloat16 [4608, 4096], P(None, 'anchor'), may hold values from -0.1875 to 0.1875
- w_key: bfloat16 [2304, 4096], P(None, 'anchor'), may hold values from -0.25 to 0.25
- w_value: bfloat16 [2304, 4096], P(None, 'anchor'), may hold values from -0.125 to 0.125
- w_out: bfloat16 [4096, 4608], P('anchor'), may hold values from -0.25 to 0.25
Outputs:
- cross_out: bfloat16 [8, 512, 4608], P('dp', ('anchor', 'aug'))
- anchor_grad: bfloat16 [8, 512, 4608], P('dp', ('anchor', 'aug'))
- aug_grad: bfloat16 [8, 512, 2304], P('dp', ('anchor', 'aug'))
- query_wgrad: float32 [4608, 4096], P(('dp', 'aug'), 'anchor')
- key_wgrad: float32 [2304, 4096], P(('dp', 'aug'), 'anchor')
- value_wgrad: float32 [2304, 4096], P(('dp', 'aug'), 'anchor')
- out_wgrad: float32 [4096, 4608], P('anchor', ('dp', 'aug'))
The draws below stay inside these ranges and needn't reach their ends.
All inputs are finite; a program needn't handle non-finite values.
Results may differ from the reference program's by a relative error of at most 0.025.
Values may be sent and summed in bfloat16 or wider, within the bound.
No kernel may reach another device: no remote copies, remote signals or barrier semaphores. Data moves between devices by JAX's collectives and lax.ppermute only.
A program may use at most 64 MiB of HBM per device.

```python
import jax
import jax.numpy as jnp
from jax import lax

D = 4608
DB = 2304
HEADS = 32
HD = 128
SEQ = 512
N_DP = 8
N_ANCHOR = 16
N_AUG = 2


def raised(values, own_key, source, target, parts, factor):
    def block_of(axis_at):
        return (jnp.arange(values.shape[axis_at]) // (values.shape[axis_at] // parts)).reshape((-1,) + (1,) * (values.ndim - 1 - axis_at))

    one_side = jax.random.permutation(own_key, parts)[block_of(target)]
    other_side = (block_of(target) + parts // 2) % parts
    return jnp.where((block_of(source) == one_side) | (block_of(source) == other_side), factor * values, values)


def block_scale(stream_key, shape, pieces, least, largest):
    def one(dim, shards_of):
        heights = jax.random.uniform(jax.random.fold_in(jax.random.fold_in(stream_key, 6), dim), (shards_of,), jnp.float32, least / len(pieces), largest / len(pieces))
        return jnp.repeat(jnp.exp(heights), shape[dim] // shards_of).reshape((-1,) + (1,) * (len(shape) - dim - 1))

    gain = one(*pieces[0])
    for cut in pieces[1:]:
        gain = gain * one(*cut)
    return gain


def noise(rng, dims, spread, limit, pieces=(), held_as=jnp.bfloat16):
    drawn = spread * jax.random.normal(rng, dims, jnp.float32)
    if pieces:
        drawn = drawn * block_scale(rng, dims, pieces, -0.22, 0.18)
    return jnp.clip(drawn, -limit, limit).astype(held_as)


def heavy_noise(stream_key, extent, deviation, bound, shards, heavy, kind=jnp.bfloat16):
    entries = deviation * jax.random.normal(stream_key, extent, jnp.float32)
    if shards:
        entries = entries * block_scale(stream_key, extent, shards, -0.22, 0.18)
    return jnp.clip(raised(entries, jax.random.fold_in(stream_key, 3), *heavy), -bound, bound).astype(kind)


def setup_inputs(seed: int = 0) -> dict:
    seeds = jax.random.split(jax.random.key(seed), 8)
    return {
        "anchor_hidden": heavy_noise(seeds[0], (N_DP, SEQ, D), 1.0, 6.0, ((0, 8), (1, 32)), (0, 2, 8, 2.0)),
        "aug_hidden": noise(seeds[1], (N_DP, SEQ, DB), 1.0, 6.0, ((0, 8), (1, 32))),
        "out_grad": noise(seeds[2], (N_DP, SEQ, D), 1.0, 6.0, ((0, 8), (1, 32))),
        "w_query": noise(seeds[3], (D, HEADS * HD), (D // 4) ** -0.5, 0.1875, ((1, 16),)),
        "w_key": noise(seeds[4], (DB, HEADS * HD), (DB // 4) ** -0.5, 0.25, ((1, 16),)),
        "w_value": noise(seeds[5], (DB, HEADS * HD), DB ** -0.5, 0.125, ((1, 16),)),
        "w_out": noise(seeds[6], (HEADS * HD, D), (HEADS * HD // 8) ** -0.5, 0.25, ((0, 16),)),
    }


SOFTCAP = 50.0
EPSILON = 1e-06

def rounded(value):
    return lax.optimization_barrier(value.astype(jnp.bfloat16)).astype(jnp.float32)

def parity_rows(array, parity):
    width = array.shape[-1]
    shaped = array.reshape(N_ANCHOR, N_AUG, SEQ // (N_ANCHOR * N_AUG), width)
    return shaped[:, parity].reshape(-1, width)

def grouped_product(pairs):
    span = HEADS // N_ANCHOR * HD
    total = None
    for group in range(N_ANCHOR):
        partial_value = None
        for left, right in pairs:
            lhs = left[:, group * span:(group + 1) * span]
            rhs = right[:, group * span:(group + 1) * span]
            term = jnp.dot(lhs, rhs.T, preferred_element_type=jnp.float32)
            partial_value = term if partial_value is None else partial_value + term
        total = rounded(partial_value) if total is None else total + rounded(partial_value)
    return total

def reference(anchor_hidden, aug_hidden, out_grad, w_query, w_key, w_value, w_out):
    score_scale = float(D // HEADS) ** (-0.5)
    position = jnp.arange(SEQ)
    causal = (position[None, :] <= position[:, None]).astype(jnp.float32)
    cross_list, anchor_list, aug_list = ([], [], [])
    query_acc = jnp.zeros((D, HEADS * HD), jnp.float32)
    key_acc = jnp.zeros((DB, HEADS * HD), jnp.float32)
    value_acc = jnp.zeros((DB, HEADS * HD), jnp.float32)
    out_acc = jnp.zeros((HEADS * HD, D), jnp.float32)
    for member in range(N_DP):
        hidden_f = anchor_hidden[member].astype(jnp.float32)
        inverse = lax.rsqrt(lax.optimization_barrier(jnp.mean(hidden_f * hidden_f, axis=1, keepdims=True)) + EPSILON)
        normal = hidden_f * inverse
        normed = normal.astype(jnp.bfloat16)
        augment = aug_hidden[member]
        query = jnp.dot(normed, w_query, preferred_element_type=jnp.float32).astype(jnp.bfloat16)
        keys = jnp.dot(augment, w_key, preferred_element_type=jnp.float32).astype(jnp.bfloat16)
        values = jnp.dot(augment, w_value, preferred_element_type=jnp.float32).astype(jnp.bfloat16)
        query_h = query.astype(jnp.float32).reshape(SEQ, HEADS, HD)
        keys_h = keys.astype(jnp.float32).reshape(SEQ, HEADS, HD)
        values_h = values.astype(jnp.float32).reshape(SEQ, HEADS, HD)
        raw_scores = jnp.einsum('ihd,jhd->hij', query_h, keys_h) * score_scale
        squashed = jnp.tanh(raw_scores / SOFTCAP)
        weighted = jnp.exp(SOFTCAP * squashed) * causal[None]
        probs = weighted / lax.optimization_barrier(jnp.sum(weighted, axis=2, keepdims=True))
        probs_b = probs.astype(jnp.bfloat16)
        attended = jnp.einsum('hij,jhd->ihd', probs_b.astype(jnp.float32), values_h)
        attended = attended.astype(jnp.bfloat16).reshape(SEQ, HEADS * HD)
        cross_list.append(grouped_product([(attended, w_out.T)]).astype(jnp.bfloat16))
        cotangent = out_grad[member]
        grad_att = jnp.dot(cotangent, w_out.T, preferred_element_type=jnp.float32).astype(jnp.bfloat16)
        grad_att_h = grad_att.astype(jnp.float32).reshape(SEQ, HEADS, HD)
        grad_probs = jnp.einsum('ihd,jhd->hij', grad_att_h, values_h)
        row_delta = lax.optimization_barrier(jnp.sum(grad_probs * probs, axis=2, keepdims=True))
        grad_scores = probs * (grad_probs - row_delta) * (1.0 - squashed * squashed) * score_scale
        grad_scores = grad_scores.astype(jnp.bfloat16).astype(jnp.float32)
        grad_query = jnp.einsum('hij,jhd->ihd', grad_scores, keys_h).astype(jnp.bfloat16).reshape(SEQ, HEADS * HD)
        grad_keys = jnp.einsum('hij,ihd->jhd', grad_scores, query_h).astype(jnp.bfloat16).reshape(SEQ, HEADS * HD)
        grad_values = jnp.einsum('hij,ihd->jhd', probs_b.astype(jnp.float32), grad_att_h)
        grad_values = grad_values.astype(jnp.bfloat16).reshape(SEQ, HEADS * HD)
        grad_normed = grouped_product([(grad_query, w_query)])
        inner = lax.optimization_barrier(jnp.mean(grad_normed * normal, axis=1, keepdims=True))
        anchor_list.append((inverse * (grad_normed - normal * inner)).astype(jnp.bfloat16))
        aug_list.append(grouped_product([(grad_keys, w_key), (grad_values, w_value)]).astype(jnp.bfloat16))
        for parity in range(N_AUG):
            normed_p = parity_rows(normed, parity)
            augment_p = parity_rows(augment, parity)
            query_acc = query_acc + rounded(jnp.dot(normed_p.T, parity_rows(grad_query, parity), preferred_element_type=jnp.float32))
            key_acc = key_acc + rounded(jnp.dot(augment_p.T, parity_rows(grad_keys, parity), preferred_element_type=jnp.float32))
            value_acc = value_acc + rounded(jnp.dot(augment_p.T, parity_rows(grad_values, parity), preferred_element_type=jnp.float32))
            out_acc = out_acc + rounded(jnp.dot(parity_rows(attended, parity).T, parity_rows(cotangent, parity), preferred_element_type=jnp.float32))
    return (jnp.stack(cross_list), jnp.stack(anchor_list), jnp.stack(aug_list), query_acc, key_acc, value_acc, out_acc)
```

```python
import jax
import jax.numpy as jnp
from jax import lax
from jax.sharding import PartitionSpec as P

D = 4608
DB = 2304
HEADS = 32
HD = 128
NZ = 8
NY = 4
F32 = jnp.float32
BF16 = jnp.bfloat16

SOFTCAP = 50.0
EPSILON = 1e-06

ORDER = (0, -1, 1, -2, 2, -3, 3, 4)


def z_shift(block, step):
    route = [(z * 2 + h, (z + step) % NZ * 2 + h) for z in range(NZ) for h in range(2)]
    return lax.ppermute(block, "anchor", route)


def x_swap(block):
    route = [(z * 2 + h, z * 2 + 1 - h) for z in range(NZ) for h in range(2)]
    return lax.ppermute(block, "anchor", route)


def y_shift(block, step):
    route = [(y * 2 + c, (y + step) % NY * 2 + c) for y in range(NY) for c in range(2)]
    return lax.ppermute(block, "dp", route)


def core_swap(block):
    route = [(y * 2 + c, y * 2 + 1 - c) for y in range(NY) for c in range(2)]
    return lax.ppermute(block, "dp", route)


def aug_swap(block):
    return lax.ppermute(block, "aug", [(0, 1), (1, 0)])


def times_transposed(left, right):
    return lax.dot_general(left, right, (((1,), (1,)), ((), ())), preferred_element_type=F32)


def transposed_times(left, right):
    return lax.dot_general(left, right, (((0,), (0,)), ((), ())), preferred_element_type=F32)


def added(*terms):
    total = terms[0].astype(F32)
    for term in terms[1:]:
        total = total + term.astype(F32)
    return total


def gather_rows(block):
    own = jnp.concatenate([block, x_swap(block)], axis=0)
    ahead = behind = own
    chunks = [own]
    for _ in range(NZ // 2 - 1):
        behind = z_shift(behind, 1)
        ahead = z_shift(ahead, -1)
        chunks += [behind, ahead]
    rows = block.shape[0]
    chunks += [z_shift(behind[:rows], 1), z_shift(ahead[rows:], -1)]
    return jnp.concatenate(chunks, axis=0)


def scatter_rows(terms):
    pair = terms.shape[0] // NZ
    rows = pair // 2

    def chunk(offset):
        at = ORDER.index(offset) * pair
        return terms[at : at + pair]

    far = chunk(NZ // 2)
    ahead = z_shift(far[:rows], 1)
    behind = z_shift(far[rows:], -1)
    up, down = chunk(3), chunk(-3)
    ahead = z_shift(jnp.concatenate([added(up[:rows], ahead).astype(BF16), up[rows:]]), 1)
    behind = z_shift(jnp.concatenate([down[:rows], added(down[rows:], behind).astype(BF16)]), -1)
    for offset in (2, 1):
        ahead = z_shift(added(chunk(offset), ahead).astype(BF16), 1)
        behind = z_shift(added(chunk(-offset), behind).astype(BF16), -1)
    near = chunk(0)
    partner = x_swap(added(near[rows:], ahead[rows:], behind[rows:]).astype(BF16))
    return added(near[:rows], ahead[:rows], behind[:rows], partner)


def scatter_weights(part):
    own_dp = lax.axis_index("dp")
    own_y, own_core = own_dp // 2, own_dp % 2
    own_aug = lax.axis_index("aug")
    rows = part.shape[0] // 16
    blocks = part.reshape(NY, 2, 2 * rows, part.shape[1])

    def pick(array, at, dim):
        return lax.dynamic_index_in_dim(array, at, dim, keepdims=False)

    received = core_swap(pick(blocks, 1 - own_core, 1))
    summed = added(pick(blocks, own_core, 1), received).astype(BF16)
    total = [pick(summed, own_y, 0)]
    for step in (1, 3, 2):
        total.append(y_shift(pick(summed, (own_y + step) % NY, 0), step))
    halves = added(*total).astype(BF16).reshape(2, rows, part.shape[1])
    return added(pick(halves, own_aug, 0), aug_swap(pick(halves, 1 - own_aug, 0)))


def body(anchor_hidden, aug_hidden, out_grad, w_query, w_key, w_value, w_out):
    score_scale = float(D // HEADS) ** (-0.5)
    block_rows = anchor_hidden.shape[1]
    row_count = block_rows * lax.axis_size("anchor")
    head_width = w_query.shape[1]
    local_heads = head_width // HD
    parity = lax.axis_index("aug")
    place = lax.axis_index("anchor")
    own_z, own_x = place // 2, place % 2

    hidden_f = anchor_hidden[0].astype(F32)
    inverse = lax.rsqrt(jnp.mean(hidden_f * hidden_f, axis=1, keepdims=True) + EPSILON)
    normal = hidden_f * inverse
    normed = normal.astype(BF16)

    rows_in = gather_rows(jnp.concatenate([aug_hidden[0], normed], axis=1))
    augment_all, normed_all = rows_in[:, :DB], rows_in[:, DB:]
    cotangent = gather_rows(out_grad[0])

    keys_own = jnp.dot(augment_all, w_key, preferred_element_type=F32).astype(BF16)
    values_own = jnp.dot(augment_all, w_value, preferred_element_type=F32).astype(BF16)
    both_own = jnp.concatenate([keys_own, values_own], axis=1)
    both = jnp.concatenate([both_own, aug_swap(both_own)], axis=0)
    keys_all, values_all = both[:, :head_width], both[:, head_width:]
    query = jnp.dot(normed_all, w_query, preferred_element_type=F32).astype(BF16)

    counter = jnp.arange(row_count, dtype=jnp.int32)
    within = counter % block_rows
    half = counter // block_rows % 2
    offset = jnp.repeat(jnp.array(ORDER, jnp.int32), 2 * block_rows)
    shard = (own_z + offset + NZ) % NZ * 2 + (own_x + half) % 2
    own_place = (shard * 2 + parity) * block_rows + within
    far_place = (shard * 2 + 1 - parity) * block_rows + within
    key_place = jnp.concatenate([own_place, far_place], axis=0)
    causal = (key_place[None, :] <= own_place[:, None]).astype(F32)

    query_h = query.reshape(row_count, local_heads, HD)
    keys_h = keys_all.reshape(2 * row_count, local_heads, HD)
    values_h = values_all.reshape(2 * row_count, local_heads, HD)
    raw_scores = (
        jnp.einsum("ihd,jhd->hij", query_h, keys_h, preferred_element_type=F32) * score_scale
    )
    squashed = jnp.tanh(raw_scores / SOFTCAP)
    weighted = jnp.exp(SOFTCAP * squashed) * causal[None]
    probs = weighted / jnp.sum(weighted, axis=2, keepdims=True)
    probs_b = probs.astype(BF16)
    attended = jnp.einsum("hij,jhd->ihd", probs_b, values_h, preferred_element_type=F32)
    attended = attended.astype(BF16).reshape(row_count, head_width)
    cross_out = scatter_rows(jnp.dot(attended, w_out, preferred_element_type=F32).astype(BF16))

    grad_att = times_transposed(cotangent, w_out).astype(BF16)
    out_wgrad = scatter_weights(transposed_times(cotangent, attended).astype(BF16)).T
    grad_att_h = grad_att.reshape(row_count, local_heads, HD)
    grad_probs = jnp.einsum("ihd,jhd->hij", grad_att_h, values_h, preferred_element_type=F32)
    row_delta = jnp.sum(grad_probs * probs, axis=2, keepdims=True)
    grad_scores = probs * (grad_probs - row_delta) * (1.0 - squashed * squashed) * score_scale
    grad_scores = grad_scores.astype(BF16)
    grad_query = jnp.einsum("hij,jhd->ihd", grad_scores, keys_h, preferred_element_type=F32)
    grad_query = grad_query.astype(BF16).reshape(row_count, head_width)
    key_terms = jnp.einsum(
        "hij,ihd->jhd", grad_scores, query_h, preferred_element_type=F32
    ).reshape(2 * row_count, head_width)
    value_terms = jnp.einsum(
        "hij,ihd->jhd", probs_b, grad_att_h, preferred_element_type=F32
    ).reshape(2 * row_count, head_width)
    terms = jnp.concatenate([key_terms, value_terms], axis=1)
    grad_both = added(terms[:row_count], aug_swap(terms[row_count:].astype(BF16))).astype(BF16)
    grad_keys, grad_values = grad_both[:, :head_width], grad_both[:, head_width:]

    normed_terms = times_transposed(grad_query, w_query).astype(BF16)
    aug_terms = (
        times_transposed(grad_keys, w_key) + times_transposed(grad_values, w_value)
    ).astype(BF16)
    rows_out = scatter_rows(jnp.concatenate([aug_terms, normed_terms], axis=1))
    aug_grad, grad_normed = rows_out[:, :DB], rows_out[:, DB:]
    inner = jnp.mean(grad_normed * normal, axis=1, keepdims=True)
    anchor_grad = inverse * (grad_normed - normal * inner)

    query_wgrad = scatter_weights(transposed_times(normed_all, grad_query).astype(BF16))
    both_wgrad = scatter_weights(transposed_times(augment_all, grad_both).astype(BF16))
    return (
        cross_out.astype(BF16)[None],
        anchor_grad.astype(BF16)[None],
        aug_grad.astype(BF16)[None],
        query_wgrad,
        both_wgrad[:, :head_width],
        both_wgrad[:, head_width:],
        out_wgrad,
    )


def solution(mesh):
    rows = P("dp", ("anchor", "aug"), None)
    columns = P(None, "anchor")
    return jax.shard_map(
        body,
        mesh=mesh,
        in_specs=(rows, rows, rows, columns, columns, columns, P("anchor", None)),
        out_specs=(
            rows,
            rows,
            rows,
            P(("dp", "aug"), "anchor"),
            P(("dp", "aug"), "anchor"),
            P(("dp", "aug"), "anchor"),
            P("anchor", ("dp", "aug")),
        ),
        check_vma=False,
    )
```

```python
import functools

import jax
import jax.numpy as jnp
from jax import lax
from jax.experimental import pallas as pl
from jax.experimental.pallas import tpu as pltpu
from jax.sharding import Mesh, PartitionSpec as P

D = 4608
DB = 2304
HEADS = 32
HD = 128
NZ = 8
NY = 4
F32 = jnp.float32
BF16 = jnp.bfloat16

SOFTCAP = 50.0
EPSILON = 1e-06


def shift(block, axis, step):
    count = lax.axis_size(axis)
    return lax.ppermute(block, axis, [(i, (i + step) % count) for i in range(count)])


def swap(block, axis):
    return lax.ppermute(block, axis, [(0, 1), (1, 0)])


def times_transposed(left, right):
    return lax.dot_general(left, right, (((1,), (1,)), ((), ())), preferred_element_type=F32)


def transposed_times(left, right):
    return lax.dot_general(left, right, (((0,), (0,)), ((), ())), preferred_element_type=F32)


def added(*terms):
    total = terms[0].astype(F32)
    for term in terms[1:]:
        total = total + term.astype(F32)
    return total


def after(value, *others):
    return lax.optimization_barrier((value, *others))[0]


def ring_gather(block, cut, wait=None):
    ahead = behind = block
    found = {0: block}
    for step in range(1, NZ // 2):
        behind = shift(behind, "z", 1)
        ahead = shift(ahead, "z", -1)
        found[NZ - step], found[step] = behind, ahead
    if wait is not None:
        ahead, behind = after((ahead, behind), wait)
    half = block.shape[cut] // 2
    low = lax.slice_in_dim(behind, 0, half, axis=cut)
    high = lax.slice_in_dim(ahead, half, 2 * half, axis=cut)
    found[NZ // 2] = jnp.concatenate([shift(low, "z", 1), shift(high, "z", -1)], axis=cut)
    rows = jnp.concatenate([found[offset] for offset in range(NZ)], axis=0)
    return rows, (found[1], found[NZ - 1])


def weights_of(q, k, causal, scale):
    raw = lax.dot_general(q, k, (((1,), (1,)), ((), ())), preferred_element_type=F32) * scale
    squashed = jnp.tanh(raw * (1.0 / SOFTCAP))
    return squashed, jnp.exp(SOFTCAP * squashed) * causal


def forward_kernel(scale, q_ref, own_ref, far_ref, causal_ref, near_ref, away_ref):
    rows, width = q_ref.shape
    for head in range(width // HD):
        keys = slice(head * HD, (head + 1) * HD)
        vals = slice(width + head * HD, width + (head + 1) * HD)
        q = q_ref[:, keys]
        _, own = weights_of(q, own_ref[:, keys], causal_ref[:, :rows], scale)
        _, far = weights_of(q, far_ref[:, keys], causal_ref[:, rows:], scale)
        total = jnp.sum(own, axis=1, keepdims=True) + jnp.sum(far, axis=1, keepdims=True)
        own, far = (own / total).astype(BF16), (far / total).astype(BF16)
        att = jnp.dot(own, own_ref[:, vals], preferred_element_type=F32)
        att = att + jnp.dot(far, far_ref[:, vals], preferred_element_type=F32)
        att = att.astype(BF16)
        block = rows // (2 * NZ)
        for index in range(2 * NZ):
            to = away_ref if index % 2 else near_ref
            at = index // 2 * block
            to[at : at + block, keys] = att[index * block : (index + 1) * block]


def backward_kernel(
    scale, q_ref, own_ref, far_ref, causal_ref, near_ref, away_ref, gq_ref, mine_ref, theirs_ref
):
    rows, width = q_ref.shape
    block = rows // (2 * NZ)
    for head in range(width // HD):
        keys = slice(head * HD, (head + 1) * HD)
        vals = slice(width + head * HD, width + (head + 1) * HD)
        q = q_ref[:, keys]
        grad = jnp.concatenate(
            [
                (away_ref if index % 2 else near_ref)[
                    index // 2 * block : (index // 2 + 1) * block, keys
                ]
                for index in range(2 * NZ)
            ],
            axis=0,
        )
        squashed, probs, grads = [], [], []
        for ref, causal in ((own_ref, causal_ref[:, :rows]), (far_ref, causal_ref[:, rows:])):
            s, w = weights_of(q, ref[:, keys], causal, scale)
            squashed.append(s)
            probs.append(w)
            grads.append(
                lax.dot_general(
                    grad, ref[:, vals], (((1,), (1,)), ((), ())), preferred_element_type=F32
                )
            )
        total = sum(jnp.sum(w, axis=1, keepdims=True) for w in probs)
        probs = [w / total for w in probs]
        delta = sum(jnp.sum(g * p, axis=1, keepdims=True) for g, p in zip(grads, probs))
        gq = jnp.zeros((rows, HD), F32)
        for ref, s, p, g, to in zip(
            (own_ref, far_ref), squashed, probs, grads, (mine_ref, theirs_ref)
        ):
            scores = (p * (g - delta) * (1.0 - s * s) * scale).astype(BF16)
            gq = gq + jnp.dot(scores, ref[:, keys], preferred_element_type=F32)
            to[:, keys] = transposed_times(scores, q).astype(to.dtype)
            to[:, vals] = transposed_times(p.astype(BF16), grad).astype(to.dtype)
        gq_ref[:, keys] = gq.astype(BF16)


def kernel_call(kernel, shapes, *args):
    return pl.pallas_call(
        kernel,
        out_shape=shapes,
        in_specs=[pl.BlockSpec(memory_space=pltpu.VMEM)] * len(args),
        out_specs=[pl.BlockSpec(memory_space=pltpu.VMEM)] * len(shapes),
        compiler_params=pltpu.CompilerParams(vmem_limit_bytes=24 * 1024 * 1024),
    )(*args)


def pick(array, at, dim):
    return lax.dynamic_index_in_dim(array, at, dim, keepdims=False)


def core_split(parts):
    own_core = lax.axis_index("core")
    blocks = [part.reshape(NY, 2, 2, part.shape[0] // 16, part.shape[1]) for part in parts]
    return tuple(
        jnp.concatenate([pick(b, core, 1) for b in blocks], axis=2)
        for core in (1 - own_core, own_core)
    )


def y_split(summed):
    own_y = lax.axis_index("y")
    return tuple(pick(summed, (own_y + step) % NY, 0) for step in (0, 1, 3, 2))


def aug_split(halves):
    own_aug = lax.axis_index("xl")
    return pick(halves, own_aug, 0), pick(halves, 1 - own_aug, 0)


def split_rows(rows, parts):
    found, at = [], 0
    for part in parts:
        found.append(rows[at : at + part.shape[0] // 16])
        at += part.shape[0] // 16
    return found


def together(*values):
    return lax.optimization_barrier(values)


def body(anchor_hidden, aug_hidden, out_grad, w_query, w_key, w_value, w_out):
    score_scale = float(D // HEADS) ** (-0.5)
    block_rows = anchor_hidden.shape[1]
    row_count = block_rows * 2 * NZ
    head_width = w_query.shape[1]
    parity = lax.axis_index("xl")
    own_z, own_x = lax.axis_index("z"), lax.axis_index("xh")

    def x_pair(block):
        return jnp.concatenate([block, swap(block, "xh")], axis=0)

    hidden_f = anchor_hidden[0].astype(F32)
    inverse = lax.rsqrt(jnp.mean(hidden_f * hidden_f, axis=1, keepdims=True) + EPSILON)
    normal = hidden_f * inverse
    rows_in = jnp.concatenate([x_pair(aug_hidden[0]), x_pair(normal.astype(BF16))], axis=1)
    rows_in, mark = ring_gather(rows_in, 0)
    cot_near, _ = ring_gather(out_grad[0], 1, mark)
    cot_away = swap(cot_near, "xh")
    augment_all, normed_all = rows_in[:, :DB], rows_in[:, DB:]

    counter = jnp.arange(row_count, dtype=jnp.int32)
    shard_z = (counter // (2 * block_rows) + own_z) % NZ
    half = (counter // block_rows + own_x) % 2
    shard = (shard_z * 2 + half) * 2
    own_place = (shard + parity) * block_rows + counter % block_rows
    far_place = (shard + 1 - parity) * block_rows + counter % block_rows
    key_place = jnp.concatenate([own_place, far_place], axis=0)
    causal = (key_place[None, :] <= own_place[:, None]).astype(F32)

    keys_own = jnp.dot(augment_all, w_key, preferred_element_type=F32).astype(BF16)
    values_own = jnp.dot(augment_all, w_value, preferred_element_type=F32).astype(BF16)
    both_own = jnp.concatenate([keys_own, values_own], axis=1)
    both_far = swap(both_own, "xl")
    query = jnp.dot(normed_all, w_query, preferred_element_type=F32).astype(BF16)

    square = jax.ShapeDtypeStruct((row_count, head_width), BF16)
    wide = (row_count, 2 * head_width)
    halfway = jax.ShapeDtypeStruct((row_count // 2, head_width), BF16)
    near, away = kernel_call(
        functools.partial(forward_kernel, score_scale),
        [halfway, halfway],
        query,
        both_own,
        both_far,
        causal,
    )
    first, last = 3 * block_rows, 6 * block_rows
    cross_away = jnp.dot(away, w_out, preferred_element_type=F32).astype(BF16)
    grad_near = times_transposed(cot_near, w_out).astype(BF16)
    out_part = transposed_times(cot_near, near) + transposed_times(cot_away, away)
    early_parts = [out_part.astype(BF16)]
    early_send, early_keep = core_split(early_parts)
    back_next = jnp.concatenate(
        [cross_away[2 * block_rows : first], cross_away[last : last + block_rows]], axis=0
    )
    back_near = jnp.concatenate(
        [cross_away[last + block_rows :], cross_away[: 2 * block_rows]], axis=0
    )
    back_far, early_send, cot_away = together(cross_away[first:last], early_send, cot_away)
    back_far = swap(back_far, "xh")
    early_sum = added(early_keep, swap(early_send, "core")).astype(BF16)
    grad_away = times_transposed(cot_away, w_out).astype(BF16)
    grad_query, mine, theirs = kernel_call(
        functools.partial(backward_kernel, score_scale),
        [square, jax.ShapeDtypeStruct(wide, F32), jax.ShapeDtypeStruct(wide, BF16)],
        query,
        both_own,
        both_far,
        causal,
        grad_near,
        grad_away,
    )
    early = y_split(early_sum)

    theirs, grad_query, mine, *early = together(theirs, grad_query, mine, *early)
    theirs = swap(theirs, "xl")
    early[1], early[2] = shift(early[1], "y", 1), shift(early[2], "y", 3)
    normed_terms = [
        times_transposed(grad_query, w_query[:DB]).astype(BF16),
        times_transposed(grad_query, w_query[DB:]).astype(BF16),
    ]
    cross_own = jnp.dot(near, w_out, preferred_element_type=F32).astype(BF16)

    theirs, back_far, cross_own, normed_terms, early = together(
        theirs, back_far, cross_own, normed_terms, early
    )
    grad_both = added(mine, theirs).astype(BF16)
    grad_keys, grad_values = grad_both[:, :head_width], grad_both[:, head_width:]
    aug_terms = times_transposed(grad_keys, w_key) + times_transposed(grad_values, w_value)
    ring_terms = jnp.stack([aug_terms.astype(BF16), *normed_terms])

    def cross_chunk(offset):
        back, at = {
            4: (back_far, 1),
            3: (back_far, 0),
            -3: (back_far, 2),
            2: (back_next, 0),
            -2: (back_next, 1),
            -1: (back_near, 0),
            0: (back_near, 1),
            1: (back_near, 2),
        }[offset]
        own = lax.slice_in_dim(cross_own, offset % NZ * block_rows, (offset % NZ + 1) * block_rows)
        terms = added(own, back[at * block_rows : (at + 1) * block_rows])
        return jnp.concatenate([terms[:, :DB], terms[:, DB:]], axis=0)[None]

    def chunk(offset):
        at = offset % NZ * 2 * block_rows
        terms = ring_terms[:, at : at + 2 * block_rows].astype(F32)
        return jnp.concatenate([terms, cross_chunk(offset)], axis=0)

    far = chunk(4).astype(BF16)
    ahead, behind = far[:, :block_rows], far[:, block_rows:]
    ahead, behind, grad_both, back_next, *early = together(
        ahead, behind, grad_both, back_next, *early
    )
    ahead, behind = shift(ahead, "z", 1), shift(behind, "z", -1)
    early[3] = shift(early[3], "y", 2)
    back_next = swap(back_next, "xh")
    both_part = transposed_times(augment_all, grad_both).astype(BF16)
    late_parts = [
        transposed_times(normed_all, grad_query).astype(BF16),
        both_part[:, :head_width],
        both_part[:, head_width:],
    ]
    late_send, late_keep = core_split(late_parts)

    ahead, behind, late_send, late_keep, back_next, *early = together(
        ahead, behind, late_send, late_keep, back_next, *early
    )
    up, down = chunk(3), chunk(-3)
    ahead = jnp.concatenate([added(up[:, :block_rows], ahead), up[:, block_rows:]], axis=1)
    behind = jnp.concatenate([down[:, :block_rows], added(down[:, block_rows:], behind)], axis=1)
    ahead, behind, late_send, back_near, *early = together(
        ahead.astype(BF16), behind.astype(BF16), late_send, back_near, *early
    )
    back_near = swap(back_near, "xh")
    ahead, behind = shift(ahead, "z", 1), shift(behind, "z", -1)
    late_sum = added(late_keep, swap(late_send, "core")).astype(BF16)
    late = y_split(late_sum)
    early_keep, early_send = aug_split(added(*early).astype(BF16))

    ahead, behind, back_near, *late = together(ahead, behind, back_near, *late)
    ahead, behind = added(chunk(2), ahead).astype(BF16), added(chunk(-2), behind).astype(BF16)
    ahead, behind, early_send, *late = together(ahead, behind, early_send, *late)
    ahead, behind = shift(ahead, "z", 1), shift(behind, "z", -1)
    late[1], late[2] = shift(late[1], "y", 1), shift(late[2], "y", 3)
    out_wgrad = added(early_keep, swap(early_send, "xl"))

    ahead, behind, out_wgrad, *late = together(ahead, behind, out_wgrad, *late)
    ahead, behind = added(chunk(1), ahead).astype(BF16), added(chunk(-1), behind).astype(BF16)
    ahead, behind, *late = together(ahead, behind, *late)
    ahead, behind = shift(ahead, "z", 1), shift(behind, "z", -1)
    late[3] = shift(late[3], "y", 2)

    ahead, behind, *late = together(ahead, behind, *late)
    sums = added(chunk(0), ahead, behind)
    theirs = sums[:3, block_rows:].astype(BF16)
    late_keep, late_send = aug_split(added(*late).astype(BF16))
    theirs, late_send = together(theirs, late_send)
    row_sums = added(sums[:3, :block_rows], swap(theirs, "xh"))
    weight_sums = added(late_keep, swap(late_send, "xl"))

    aug_grad = row_sums[0]
    grad_normed = jnp.concatenate([row_sums[1], row_sums[2]], axis=1)
    inner = jnp.mean(grad_normed * normal, axis=1, keepdims=True)
    anchor_grad = inverse * (grad_normed - normal * inner)
    cross_out = jnp.concatenate([sums[3, :block_rows], sums[3, block_rows:]], axis=1)
    query_wgrad, key_wgrad, value_wgrad = split_rows(weight_sums, late_parts)
    return (
        cross_out.astype(BF16)[None],
        anchor_grad.astype(BF16)[None],
        aug_grad.astype(BF16)[None],
        query_wgrad,
        key_wgrad,
        value_wgrad,
        out_wgrad.T,
    )


def solution(mesh):
    fine = Mesh(mesh.devices.reshape(NY, 2, NZ, 2, 2), ("y", "core", "z", "xh", "xl"))
    rows = P(("y", "core"), ("z", "xh", "xl"), None)
    columns = P(None, ("z", "xh"))
    return jax.shard_map(
        body,
        mesh=fine,
        in_specs=(rows, rows, rows, columns, columns, columns, P(("z", "xh"), None)),
        out_specs=(
            rows,
            rows,
            rows,
            P(("y", "core", "xl"), ("z", "xh")),
            P(("y", "core", "xl"), ("z", "xh")),
            P(("y", "core", "xl"), ("z", "xh")),
            P(("z", "xh"), ("y", "core", "xl")),
        ),
        check_vma=False,
    )
```

```python
import functools

import jax
import jax.numpy as jnp
from jax import lax
from jax.experimental import pallas as pl
from jax.experimental.pallas import tpu as pltpu
from jax.sharding import Mesh, PartitionSpec as P

D = 4608
DB = 2304
HEADS = 32
HD = 128
NZ = 8
NY = 4
F32 = jnp.float32
BF16 = jnp.bfloat16

SOFTCAP = 50.0
EPSILON = 1e-06


def shift(block, axis, step):
    count = lax.axis_size(axis)
    return lax.ppermute(block, axis, [(i, (i + step) % count) for i in range(count)])


def swap(block, axis):
    return lax.ppermute(block, axis, [(0, 1), (1, 0)])


def times_transposed(left, right):
    return lax.dot_general(left, right, (((1,), (1,)), ((), ())), preferred_element_type=F32)


def transposed_times(left, right):
    return lax.dot_general(left, right, (((0,), (0,)), ((), ())), preferred_element_type=F32)


def added(*terms):
    total = terms[0].astype(F32)
    for term in terms[1:]:
        total = total + term.astype(F32)
    return total


def after(value, *others):
    return lax.optimization_barrier((value, *others))[0]


def rows_of(found):
    return jnp.concatenate([found[offset] for offset in range(NZ)], axis=0)


def weights_of(q, k, causal, scale):
    raw = lax.dot_general(q, k, (((1,), (1,)), ((), ())), preferred_element_type=F32) * scale
    squashed = jnp.tanh(raw * (1.0 / SOFTCAP))
    return squashed, jnp.exp(SOFTCAP * squashed) * causal


def forward_kernel(scale, q_ref, own_ref, far_ref, causal_ref, near_ref, away_ref):
    rows, width = q_ref.shape
    for head in range(width // HD):
        keys = slice(head * HD, (head + 1) * HD)
        vals = slice(width + head * HD, width + (head + 1) * HD)
        q = q_ref[:, keys]
        _, own = weights_of(q, own_ref[:, keys], causal_ref[:, :rows], scale)
        _, far = weights_of(q, far_ref[:, keys], causal_ref[:, rows:], scale)
        total = jnp.sum(own, axis=1, keepdims=True) + jnp.sum(far, axis=1, keepdims=True)
        own, far = (own / total).astype(BF16), (far / total).astype(BF16)
        att = jnp.dot(own, own_ref[:, vals], preferred_element_type=F32)
        att = att + jnp.dot(far, far_ref[:, vals], preferred_element_type=F32)
        att = att.astype(BF16)
        block = rows // (2 * NZ)
        for index in range(2 * NZ):
            to = away_ref if index % 2 else near_ref
            at = index // 2 * block
            to[at : at + block, keys] = att[index * block : (index + 1) * block]


def backward_kernel(
    scale, q_ref, own_ref, far_ref, causal_ref, near_ref, away_ref, gq_ref, mine_ref, theirs_ref
):
    rows, width = q_ref.shape
    block = rows // (2 * NZ)
    for head in range(width // HD):
        keys = slice(head * HD, (head + 1) * HD)
        vals = slice(width + head * HD, width + (head + 1) * HD)
        q = q_ref[:, keys]
        grad = jnp.concatenate(
            [
                (away_ref if index % 2 else near_ref)[
                    index // 2 * block : (index // 2 + 1) * block, keys
                ]
                for index in range(2 * NZ)
            ],
            axis=0,
        )
        squashed, probs, grads = [], [], []
        for ref, causal in ((own_ref, causal_ref[:, :rows]), (far_ref, causal_ref[:, rows:])):
            s, w = weights_of(q, ref[:, keys], causal, scale)
            squashed.append(s)
            probs.append(w)
            grads.append(
                lax.dot_general(
                    grad, ref[:, vals], (((1,), (1,)), ((), ())), preferred_element_type=F32
                )
            )
        total = sum(jnp.sum(w, axis=1, keepdims=True) for w in probs)
        probs = [w / total for w in probs]
        delta = sum(jnp.sum(g * p, axis=1, keepdims=True) for g, p in zip(grads, probs))
        gq = jnp.zeros((rows, HD), F32)
        for ref, s, p, g, to in zip(
            (own_ref, far_ref), squashed, probs, grads, (mine_ref, theirs_ref)
        ):
            scores = (p * (g - delta) * (1.0 - s * s) * scale).astype(BF16)
            gq = gq + jnp.dot(scores, ref[:, keys], preferred_element_type=F32)
            to[:, keys] = transposed_times(scores, q).astype(to.dtype)
            to[:, vals] = transposed_times(p.astype(BF16), grad).astype(to.dtype)
        gq_ref[:, keys] = gq.astype(BF16)


def kernel_call(kernel, shapes, *args):
    return pl.pallas_call(
        kernel,
        out_shape=shapes,
        in_specs=[pl.BlockSpec(memory_space=pltpu.VMEM)] * len(args),
        out_specs=[pl.BlockSpec(memory_space=pltpu.VMEM)] * len(shapes),
        compiler_params=pltpu.CompilerParams(vmem_limit_bytes=24 * 1024 * 1024),
    )(*args)


def pick(array, at, dim):
    return lax.dynamic_index_in_dim(array, at, dim, keepdims=False)


def core_split(parts):
    own_core = lax.axis_index("core")
    blocks = [part.reshape(NY, 2, 2, part.shape[0] // 16, part.shape[1]) for part in parts]
    return tuple(
        jnp.concatenate([pick(b, core, 1) for b in blocks], axis=2)
        for core in (1 - own_core, own_core)
    )


def y_split(summed):
    own_y = lax.axis_index("y")
    return tuple(pick(summed, (own_y + step) % NY, 0) for step in (0, 1, 3, 2))


def aug_split(halves):
    own_aug = lax.axis_index("xl")
    return pick(halves, own_aug, 0), pick(halves, 1 - own_aug, 0)


def split_rows(rows, parts):
    found, at = [], 0
    for part in parts:
        found.append(rows[at : at + part.shape[0] // 16])
        at += part.shape[0] // 16
    return found


def together(*values):
    return lax.optimization_barrier(values)


def body(anchor_hidden, aug_hidden, out_grad, w_query, w_key, w_value, w_out):
    score_scale = float(D // HEADS) ** (-0.5)
    block_rows = anchor_hidden.shape[1]
    row_count = block_rows * 2 * NZ
    head_width = w_query.shape[1]
    parity = lax.axis_index("xl")
    own_z, own_x = lax.axis_index("z"), lax.axis_index("xh")

    def x_pair(block):
        return jnp.concatenate([block, swap(block, "xh")], axis=0)

    hidden_f = anchor_hidden[0].astype(F32)
    inverse = lax.rsqrt(jnp.mean(hidden_f * hidden_f, axis=1, keepdims=True) + EPSILON)
    normal = hidden_f * inverse
    rows_in = jnp.concatenate([x_pair(aug_hidden[0]), x_pair(normal.astype(BF16))], axis=1)

    rings = [(rows_in, rows_in), (out_grad[0], out_grad[0])]
    found = [{0: rows_in}, {0: out_grad[0]}]

    def step(ring, number):
        rings[ring] = (shift(rings[ring][0], "z", 1), shift(rings[ring][1], "z", -1))
        found[ring][NZ - number], found[ring][number] = rings[ring]

    def last_step(ring, cut):
        behind, ahead = rings[ring]
        half = behind.shape[cut] // 2
        low = lax.slice_in_dim(behind, 0, half, axis=cut)
        high = lax.slice_in_dim(ahead, half, 2 * half, axis=cut)
        halves = [shift(low, "z", 1), shift(high, "z", -1)]
        found[ring][NZ // 2] = jnp.concatenate(halves, axis=cut)

    step(1, 1)
    step(0, 1)
    step(1, 2)
    cot_sent = jnp.concatenate([found[1][offset] for offset in (6, 7, 0, 1, 2)], axis=0)
    rings[1], rings[0], cot_sent = together(rings[1], rings[0], cot_sent)
    cot_first = swap(cot_sent, "xh")
    step(0, 2)
    step(1, 3)
    last_step(1, 1)
    cot_sent = jnp.concatenate([found[1][offset] for offset in (3, 4, 5)], axis=0)
    rings[0], cot_sent = together(rings[0], cot_sent)
    step(0, 3)
    rings[0], cot_first = together(rings[0], cot_first)
    cot_second = swap(cot_sent, "xh")
    last_step(0, 0)
    rows_in, cot_near = rows_of(found[0]), rows_of(found[1])
    cot_away = jnp.concatenate(
        [cot_first[2 * block_rows :], cot_second, cot_first[: 2 * block_rows]], axis=0
    )
    augment_all, normed_all = rows_in[:, :DB], rows_in[:, DB:]

    counter = jnp.arange(row_count, dtype=jnp.int32)
    shard_z = (counter // (2 * block_rows) + own_z) % NZ
    half = (counter // block_rows + own_x) % 2
    shard = (shard_z * 2 + half) * 2
    own_place = (shard + parity) * block_rows + counter % block_rows
    far_place = (shard + 1 - parity) * block_rows + counter % block_rows
    key_place = jnp.concatenate([own_place, far_place], axis=0)
    causal = (key_place[None, :] <= own_place[:, None]).astype(F32)

    keys_own = jnp.dot(augment_all, w_key, preferred_element_type=F32).astype(BF16)
    values_own = jnp.dot(augment_all, w_value, preferred_element_type=F32).astype(BF16)
    both_own = jnp.concatenate([keys_own, values_own], axis=1)
    both_far = swap(both_own, "xl")
    query = jnp.dot(normed_all, w_query, preferred_element_type=F32).astype(BF16)

    square = jax.ShapeDtypeStruct((row_count, head_width), BF16)
    wide = (row_count, 2 * head_width)
    halfway = jax.ShapeDtypeStruct((row_count // 2, head_width), BF16)
    near, away = kernel_call(
        functools.partial(forward_kernel, score_scale),
        [halfway, halfway],
        query,
        both_own,
        both_far,
        causal,
    )
    grad_near = times_transposed(cot_near, w_out).astype(BF16)
    grad_away = times_transposed(cot_away, w_out).astype(BF16)
    grad_query, mine, theirs = kernel_call(
        functools.partial(backward_kernel, score_scale),
        [square, jax.ShapeDtypeStruct(wide, F32), jax.ShapeDtypeStruct(wide, BF16)],
        query,
        both_own,
        both_far,
        causal,
        grad_near,
        grad_away,
    )

    def cross_of(rows):
        sides = [w_out[:, :DB], w_out[:, DB:]]
        return jnp.stack(
            [jnp.dot(rows, side, preferred_element_type=F32).astype(BF16) for side in sides]
        )

    def cross_block(array, offset):
        return array[:, offset % NZ * block_rows :][:, :block_rows]

    def cross_sent(*offsets):
        return jnp.concatenate([cross_block(cross_away, offset) for offset in offsets], axis=1)

    theirs, grad_query, mine, near, away = together(theirs, grad_query, mine, near, away)
    theirs = swap(theirs, "xl")
    cross_away = cross_of(away)
    back = {offsets: cross_sent(*offsets) for offsets in ((4,), (3, -3), (2, -2), (1, -1, 0))}
    early_parts = [
        (transposed_times(cot_near, near) + transposed_times(cot_away, away)).astype(BF16)
    ]
    early_send, early_keep = core_split(early_parts)
    theirs, back, grad_query, near, early_keep, early_send = together(
        theirs, back, grad_query, near, early_keep, early_send
    )

    back[4,] = swap(back[4,], "xh")
    early_sum = added(early_keep, swap(early_send, "core")).astype(BF16)
    cross_own = cross_of(near)
    normed_terms = [
        times_transposed(grad_query, w_query[:DB]).astype(BF16),
        times_transposed(grad_query, w_query[DB:]).astype(BF16),
    ]
    grad_both = added(mine, theirs).astype(BF16)
    grad_keys, grad_values = grad_both[:, :head_width], grad_both[:, head_width:]
    aug_terms = times_transposed(grad_keys, w_key) + times_transposed(grad_values, w_value)
    ring_terms = jnp.stack([aug_terms.astype(BF16), *normed_terms])
    both_part = transposed_times(augment_all, grad_both).astype(BF16)
    late_parts = [
        transposed_times(normed_all, grad_query).astype(BF16),
        both_part[:, :head_width],
        both_part[:, head_width:],
    ]
    late_send, late_keep = core_split(late_parts)
    early = list(y_split(early_sum))

    def chunks(*offsets):
        found = []
        for index, offset in enumerate(offsets):
            at = offset % NZ * 2 * block_rows
            received = back[offsets][:, index * block_rows : (index + 1) * block_rows]
            cross = added(cross_block(cross_own, offset), received).astype(BF16)
            cross = cross.reshape(1, 2 * block_rows, DB)
            found.append(jnp.concatenate([ring_terms[:, at : at + 2 * block_rows], cross], axis=0))
        return found

    (far,) = chunks(4)
    ahead, behind = far[:, :block_rows], far[:, block_rows:]
    ahead, behind, late_send, late_keep, back, early = together(
        ahead, behind, late_send, late_keep, back, early
    )
    ahead, behind = shift(ahead, "z", 1), shift(behind, "z", -1)
    back[3, -3] = swap(back[3, -3], "xh")
    late_back = swap(late_send, "core")
    early[3] = shift(early[3], "y", 2)
    up, down = chunks(3, -3)

    ahead, behind, up, down, back, late_keep, late_back, early = together(
        ahead, behind, up, down, back, late_keep, late_back, early
    )
    ahead = jnp.concatenate(
        [added(up[:, :block_rows], ahead).astype(BF16), up[:, block_rows:]], axis=1
    )
    behind = jnp.concatenate(
        [down[:, :block_rows], added(down[:, block_rows:], behind).astype(BF16)], axis=1
    )
    ahead, behind, back, late_keep, late_back, early = together(
        ahead, behind, back, late_keep, late_back, early
    )
    ahead, behind = shift(ahead, "z", 1), shift(behind, "z", -1)
    back[2, -2] = swap(back[2, -2], "xh")
    early[1], early[2] = shift(early[1], "y", 1), shift(early[2], "y", 3)
    late = list(y_split(added(late_keep, late_back).astype(BF16)))
    up, down = chunks(2, -2)

    ahead, behind, up, down, back, early, late = together(
        ahead, behind, up, down, back, early, late
    )
    ahead, behind = added(up, ahead).astype(BF16), added(down, behind).astype(BF16)
    ahead, behind, back, early, late = together(ahead, behind, back, early, late)
    ahead, behind = shift(ahead, "z", 1), shift(behind, "z", -1)
    back[1, -1, 0] = swap(back[1, -1, 0], "xh")
    late[1], late[2] = shift(late[1], "y", 1), shift(late[2], "y", 3)
    early_keep, early_send = aug_split(added(*early).astype(BF16))
    up, down, near = chunks(1, -1, 0)

    ahead, behind, up, down, near, early_keep, early_send, late = together(
        ahead, behind, up, down, near, early_keep, early_send, late
    )
    ahead, behind = added(up, ahead).astype(BF16), added(down, behind).astype(BF16)
    ahead, behind, near, early_send, late = together(ahead, behind, near, early_send, late)
    ahead, behind = shift(ahead, "z", 1), shift(behind, "z", -1)
    late[3] = shift(late[3], "y", 2)
    out_wgrad = added(early_keep, swap(early_send, "xl"))

    ahead, behind, out_wgrad, late = together(ahead, behind, out_wgrad, late)
    theirs = added(*(part[:3, block_rows:] for part in (near, ahead, behind))).astype(BF16)
    late_keep, late_send = aug_split(added(*late).astype(BF16))
    theirs, late_send, near, ahead, behind = together(theirs, late_send, near, ahead, behind)
    theirs, late_send = swap(theirs, "xh"), swap(late_send, "xl")
    weight_sums = [
        added(keep, sent)
        for keep, sent in zip(split_rows(late_keep, late_parts), split_rows(late_send, late_parts))
    ]
    theirs, weight_sums = together(theirs, weight_sums)
    row_sums = added(*(part[:3, :block_rows] for part in (near, ahead, behind)), theirs)
    cross_sums = added(near[3], ahead[3], behind[3])

    aug_grad = row_sums[0]
    grad_normed = jnp.concatenate([row_sums[1], row_sums[2]], axis=1)
    inner = jnp.mean(grad_normed * normal, axis=1, keepdims=True)
    anchor_grad = inverse * (grad_normed - normal * inner)
    cross_out = jnp.concatenate([cross_sums[:block_rows], cross_sums[block_rows:]], axis=1)
    query_wgrad, key_wgrad, value_wgrad = weight_sums
    return (
        cross_out.astype(BF16)[None],
        anchor_grad.astype(BF16)[None],
        aug_grad.astype(BF16)[None],
        query_wgrad,
        key_wgrad,
        value_wgrad,
        out_wgrad.T,
    )


def solution(mesh):
    fine = Mesh(mesh.devices.reshape(NY, 2, NZ, 2, 2), ("y", "core", "z", "xh", "xl"))
    rows = P(("y", "core"), ("z", "xh", "xl"), None)
    columns = P(None, ("z", "xh"))
    return jax.shard_map(
        body,
        mesh=fine,
        in_specs=(rows, rows, rows, columns, columns, columns, P(("z", "xh"), None)),
        out_specs=(
            rows,
            rows,
            rows,
            P(("y", "core", "xl"), ("z", "xh")),
            P(("y", "core", "xl"), ("z", "xh")),
            P(("y", "core", "xl"), ("z", "xh")),
            P(("z", "xh"), ("y", "core", "xl")),
        ),
        check_vma=False,
    )
```

```python
import functools

import jax
import jax.numpy as jnp
from jax import lax
from jax.experimental import pallas as pl
from jax.experimental.pallas import tpu as pltpu
from jax.sharding import Mesh, PartitionSpec as P

D = 4608
DB = 2304
HEADS = 32
HD = 128
NZ = 8
NY = 4
F32 = jnp.float32
BF16 = jnp.bfloat16

SOFTCAP = 50.0
EPSILON = 1e-06


def shift(block, axis, step):
    count = lax.axis_size(axis)
    return lax.ppermute(block, axis, [(i, (i + step) % count) for i in range(count)])


def swap(block, axis):
    return lax.ppermute(block, axis, [(0, 1), (1, 0)])


def times_transposed(left, right):
    return lax.dot_general(left, right, (((1,), (1,)), ((), ())), preferred_element_type=F32)


def transposed_times(left, right):
    return lax.dot_general(left, right, (((0,), (0,)), ((), ())), preferred_element_type=F32)


def added(*terms):
    total = terms[0].astype(F32)
    for term in terms[1:]:
        total = total + term.astype(F32)
    return total


def after(value, *others):
    return lax.optimization_barrier((value, *others))[0]


def rows_of(found):
    return jnp.concatenate([found[offset] for offset in range(NZ)], axis=0)


def weights_of(q, k, causal, scale):
    raw = lax.dot_general(q, k, (((1,), (1,)), ((), ())), preferred_element_type=F32) * scale
    squashed = jnp.tanh(raw * (1.0 / SOFTCAP))
    return squashed, jnp.exp(SOFTCAP * squashed) * causal


def forward_kernel(scale, q_ref, own_ref, far_ref, causal_ref, near_ref, away_ref):
    rows, width = q_ref.shape
    for head in range(width // HD):
        keys = slice(head * HD, (head + 1) * HD)
        vals = slice(width + head * HD, width + (head + 1) * HD)
        q = q_ref[:, keys]
        _, own = weights_of(q, own_ref[:, keys], causal_ref[:, :rows], scale)
        _, far = weights_of(q, far_ref[:, keys], causal_ref[:, rows:], scale)
        total = jnp.sum(own, axis=1, keepdims=True) + jnp.sum(far, axis=1, keepdims=True)
        own, far = (own / total).astype(BF16), (far / total).astype(BF16)
        att = jnp.dot(own, own_ref[:, vals], preferred_element_type=F32)
        att = att + jnp.dot(far, far_ref[:, vals], preferred_element_type=F32)
        att = att.astype(BF16)
        block = rows // (2 * NZ)
        for index in range(2 * NZ):
            to = away_ref if index % 2 else near_ref
            at = index // 2 * block
            to[at : at + block, keys] = att[index * block : (index + 1) * block]


def backward_kernel(
    scale, q_ref, own_ref, far_ref, causal_ref, near_ref, away_ref, gq_ref, mine_ref, theirs_ref
):
    rows, width = q_ref.shape
    block = rows // (2 * NZ)
    for head in range(width // HD):
        keys = slice(head * HD, (head + 1) * HD)
        vals = slice(width + head * HD, width + (head + 1) * HD)
        q = q_ref[:, keys]
        grad = jnp.concatenate(
            [
                (away_ref if index % 2 else near_ref)[
                    index // 2 * block : (index // 2 + 1) * block, keys
                ]
                for index in range(2 * NZ)
            ],
            axis=0,
        )
        squashed, probs, grads = [], [], []
        for ref, causal in ((own_ref, causal_ref[:, :rows]), (far_ref, causal_ref[:, rows:])):
            s, w = weights_of(q, ref[:, keys], causal, scale)
            squashed.append(s)
            probs.append(w)
            grads.append(
                lax.dot_general(
                    grad, ref[:, vals], (((1,), (1,)), ((), ())), preferred_element_type=F32
                )
            )
        total = sum(jnp.sum(w, axis=1, keepdims=True) for w in probs)
        probs = [w / total for w in probs]
        delta = sum(jnp.sum(g * p, axis=1, keepdims=True) for g, p in zip(grads, probs))
        gq = jnp.zeros((rows, HD), F32)
        for ref, s, p, g, to in zip(
            (own_ref, far_ref), squashed, probs, grads, (mine_ref, theirs_ref)
        ):
            scores = (p * (g - delta) * (1.0 - s * s) * scale).astype(BF16)
            gq = gq + jnp.dot(scores, ref[:, keys], preferred_element_type=F32)
            to[:, keys] = transposed_times(scores, q).astype(to.dtype)
            to[:, vals] = transposed_times(p.astype(BF16), grad).astype(to.dtype)
        gq_ref[:, keys] = gq.astype(BF16)


def kernel_call(kernel, shapes, *args):
    return pl.pallas_call(
        kernel,
        out_shape=shapes,
        in_specs=[pl.BlockSpec(memory_space=pltpu.VMEM)] * len(args),
        out_specs=[pl.BlockSpec(memory_space=pltpu.VMEM)] * len(shapes),
        compiler_params=pltpu.CompilerParams(vmem_limit_bytes=24 * 1024 * 1024),
    )(*args)


def pick(array, at, dim):
    return lax.dynamic_index_in_dim(array, at, dim, keepdims=False)


def core_split(parts):
    own_core = lax.axis_index("core")
    blocks = [part.reshape(NY, 2, 2, part.shape[0] // 16, part.shape[1]) for part in parts]
    return tuple(
        jnp.concatenate([pick(b, core, 1) for b in blocks], axis=2)
        for core in (1 - own_core, own_core)
    )


def y_split(summed):
    own_y = lax.axis_index("y")
    return tuple(pick(summed, (own_y + step) % NY, 0) for step in (0, 1, 3, 2))


def aug_split(halves):
    own_aug = lax.axis_index("xl")
    return pick(halves, own_aug, 0), pick(halves, 1 - own_aug, 0)


def split_rows(rows, parts):
    found, at = [], 0
    for part in parts:
        found.append(rows[at : at + part.shape[0] // 16])
        at += part.shape[0] // 16
    return found


def together(*values):
    return lax.optimization_barrier(values)


def body(anchor_hidden, aug_hidden, out_grad, w_query, w_key, w_value, w_out):
    score_scale = float(D // HEADS) ** (-0.5)
    block_rows = anchor_hidden.shape[1]
    row_count = block_rows * 2 * NZ
    head_width = w_query.shape[1]
    parity = lax.axis_index("xl")
    own_z, own_x = lax.axis_index("z"), lax.axis_index("xh")

    def x_pair(block):
        return jnp.concatenate([block, swap(block, "xh")], axis=0)

    hidden_f = anchor_hidden[0].astype(F32)
    inverse = lax.rsqrt(jnp.mean(hidden_f * hidden_f, axis=1, keepdims=True) + EPSILON)
    normal = hidden_f * inverse
    rows_in = jnp.concatenate([x_pair(aug_hidden[0]), x_pair(normal.astype(BF16))], axis=1)

    rings = [(rows_in, rows_in), (out_grad[0], out_grad[0])]
    found = [{0: rows_in}, {0: out_grad[0]}]

    def step(ring, number):
        rings[ring] = (shift(rings[ring][0], "z", 1), shift(rings[ring][1], "z", -1))
        found[ring][NZ - number], found[ring][number] = rings[ring]

    def last_step(ring, cut):
        behind, ahead = rings[ring]
        half = behind.shape[cut] // 2
        low = lax.slice_in_dim(behind, 0, half, axis=cut)
        high = lax.slice_in_dim(ahead, half, 2 * half, axis=cut)
        halves = [shift(low, "z", 1), shift(high, "z", -1)]
        found[ring][NZ // 2] = jnp.concatenate(halves, axis=cut)

    step(1, 1)
    step(0, 1)
    step(1, 2)
    cot_sent = jnp.concatenate([found[1][offset] for offset in (6, 7, 0, 1, 2)], axis=0)
    rings[1], rings[0], cot_sent = together(rings[1], rings[0], cot_sent)
    cot_first = swap(cot_sent, "xh")
    step(0, 2)
    step(1, 3)
    last_step(1, 1)
    cot_sent = jnp.concatenate([found[1][offset] for offset in (3, 4, 5)], axis=0)
    rings[0], cot_sent = together(rings[0], cot_sent)
    step(0, 3)
    rings[0], cot_first = together(rings[0], cot_first)
    cot_second = swap(cot_sent, "xh")
    last_step(0, 0)
    rows_in, cot_near = rows_of(found[0]), rows_of(found[1])
    cot_away = jnp.concatenate(
        [cot_first[2 * block_rows :], cot_second, cot_first[: 2 * block_rows]], axis=0
    )
    augment_all, normed_all = rows_in[:, :DB], rows_in[:, DB:]

    counter = jnp.arange(row_count, dtype=jnp.int32)
    shard_z = (counter // (2 * block_rows) + own_z) % NZ
    half = (counter // block_rows + own_x) % 2
    shard = (shard_z * 2 + half) * 2
    own_place = (shard + parity) * block_rows + counter % block_rows
    far_place = (shard + 1 - parity) * block_rows + counter % block_rows
    key_place = jnp.concatenate([own_place, far_place], axis=0)
    causal = (key_place[None, :] <= own_place[:, None]).astype(F32)

    keys_own = jnp.dot(augment_all, w_key, preferred_element_type=F32).astype(BF16)
    values_own = jnp.dot(augment_all, w_value, preferred_element_type=F32).astype(BF16)
    both_own = jnp.concatenate([keys_own, values_own], axis=1)
    both_far = swap(both_own, "xl")
    query = jnp.dot(normed_all, w_query, preferred_element_type=F32).astype(BF16)

    square = jax.ShapeDtypeStruct((row_count, head_width), BF16)
    wide = (row_count, 2 * head_width)
    halfway = jax.ShapeDtypeStruct((row_count // 2, head_width), BF16)
    near, away = kernel_call(
        functools.partial(forward_kernel, score_scale),
        [halfway, halfway],
        query,
        both_own,
        both_far,
        causal,
    )
    def cross_of(rows):
        sides = [w_out[:, :DB], w_out[:, DB:]]
        return jnp.stack(
            [jnp.dot(rows, side, preferred_element_type=F32).astype(BF16) for side in sides]
        )

    def cross_block(array, offset):
        return array[:, offset % NZ * block_rows :][:, :block_rows]

    def cross_sent(*offsets):
        return jnp.concatenate([cross_block(cross_away, offset) for offset in offsets], axis=1)

    cross_away = cross_of(away)
    back = {(4,): cross_block(cross_away, 4)}
    grad_near = times_transposed(cot_near, w_out).astype(BF16)
    grad_away = times_transposed(cot_away, w_out).astype(BF16)
    grad_query, mine, theirs = kernel_call(
        functools.partial(backward_kernel, score_scale),
        [square, jax.ShapeDtypeStruct(wide, F32), jax.ShapeDtypeStruct(wide, BF16)],
        query,
        both_own,
        both_far,
        causal,
        grad_near,
        grad_away,
    )

    theirs, grad_query, mine, near, away, back, cross_away = together(
        theirs, grad_query, mine, near, away, back, cross_away
    )
    theirs = swap(theirs, "xl")
    back[4,] = swap(back[4,], "xh")
    cross_own = cross_of(near)
    normed_terms = [
        times_transposed(grad_query, w_query[:DB]).astype(BF16),
        times_transposed(grad_query, w_query[DB:]).astype(BF16),
    ]
    for offsets in ((3, -3), (2, -2), (1, -1, 0)):
        back[offsets] = cross_sent(*offsets)
    theirs, back, cross_own, normed_terms, near, away = together(
        theirs, back, cross_own, normed_terms, near, away
    )
    grad_both = added(mine, theirs).astype(BF16)
    grad_keys, grad_values = grad_both[:, :head_width], grad_both[:, head_width:]
    aug_terms = times_transposed(grad_keys, w_key) + times_transposed(grad_values, w_value)
    ring_terms = jnp.stack([aug_terms.astype(BF16), *normed_terms])

    def chunks(*offsets):
        found = []
        for offset in offsets:
            at = offset % NZ * 2 * block_rows
            sent = next(sent for sent in back if offset in sent)
            received = back[sent][:, sent.index(offset) * block_rows :][:, :block_rows]
            cross = added(cross_block(cross_own, offset), received).astype(BF16)
            cross = cross.reshape(1, 2 * block_rows, DB)
            found.append(jnp.concatenate([ring_terms[:, at : at + 2 * block_rows], cross], axis=0))
        return found

    (far,) = chunks(4)
    ahead, behind = far[:, :block_rows], far[:, block_rows:]
    ahead, behind, back, grad_both, near, away = together(
        ahead, behind, back, grad_both, near, away
    )
    ahead, behind = shift(ahead, "z", 1), shift(behind, "z", -1)
    back[3, -3] = swap(back[3, -3], "xh")
    early_parts = [
        (transposed_times(cot_near, near) + transposed_times(cot_away, away)).astype(BF16)
    ]
    early_send, early_keep = core_split(early_parts)
    early = list(y_split(added(early_keep, swap(early_send, "core")).astype(BF16)))
    both_part = transposed_times(augment_all, grad_both).astype(BF16)
    late_parts = [
        transposed_times(normed_all, grad_query).astype(BF16),
        both_part[:, :head_width],
        both_part[:, head_width:],
    ]
    late_send, late_keep = core_split(late_parts)
    late_back = swap(late_send, "core")
    up, down = chunks(3, -3)

    ahead, behind, up, down, back, late_keep, late_back, early = together(
        ahead, behind, up, down, back, late_keep, late_back, early
    )
    ahead = jnp.concatenate(
        [added(up[:, :block_rows], ahead).astype(BF16), up[:, block_rows:]], axis=1
    )
    behind = jnp.concatenate(
        [down[:, :block_rows], added(down[:, block_rows:], behind).astype(BF16)], axis=1
    )
    ahead, behind, back, late_keep, late_back, early = together(
        ahead, behind, back, late_keep, late_back, early
    )
    ahead, behind = shift(ahead, "z", 1), shift(behind, "z", -1)
    back[2, -2] = swap(back[2, -2], "xh")
    early[1], early[2] = shift(early[1], "y", 1), shift(early[2], "y", 3)
    early[3] = shift(after(early[3], early[1]), "y", 2)
    late = list(y_split(added(late_keep, late_back).astype(BF16)))
    up, down = chunks(2, -2)

    ahead, behind, up, down, back, early, late = together(
        ahead, behind, up, down, back, early, late
    )
    ahead, behind = added(up, ahead).astype(BF16), added(down, behind).astype(BF16)
    ahead, behind, back, early, late = together(ahead, behind, back, early, late)
    ahead, behind = shift(ahead, "z", 1), shift(behind, "z", -1)
    back[1, -1, 0] = swap(back[1, -1, 0], "xh")
    late[1], late[2] = shift(late[1], "y", 1), shift(late[2], "y", 3)
    early_keep, early_send = aug_split(added(*early).astype(BF16))
    up, down, near = chunks(1, -1, 0)

    ahead, behind, up, down, near, early_keep, early_send, late = together(
        ahead, behind, up, down, near, early_keep, early_send, late
    )
    ahead, behind = added(up, ahead).astype(BF16), added(down, behind).astype(BF16)
    ahead, behind, near, early_send, late = together(ahead, behind, near, early_send, late)
    ahead, behind = shift(ahead, "z", 1), shift(behind, "z", -1)
    late[3] = shift(late[3], "y", 2)
    out_wgrad = added(early_keep, swap(early_send, "xl"))

    ahead, behind, out_wgrad, late = together(ahead, behind, out_wgrad, late)
    theirs = added(*(part[:3, block_rows:] for part in (near, ahead, behind))).astype(BF16)
    late_keep, late_send = aug_split(added(*late).astype(BF16))
    theirs, late_send, near, ahead, behind = together(theirs, late_send, near, ahead, behind)
    theirs, late_send = swap(theirs, "xh"), swap(late_send, "xl")
    weight_sums = [
        added(keep, sent)
        for keep, sent in zip(split_rows(late_keep, late_parts), split_rows(late_send, late_parts))
    ]
    theirs, weight_sums = together(theirs, weight_sums)
    row_sums = added(*(part[:3, :block_rows] for part in (near, ahead, behind)), theirs)
    cross_sums = added(near[3], ahead[3], behind[3])

    aug_grad = row_sums[0]
    grad_normed = jnp.concatenate([row_sums[1], row_sums[2]], axis=1)
    inner = jnp.mean(grad_normed * normal, axis=1, keepdims=True)
    anchor_grad = inverse * (grad_normed - normal * inner)
    cross_out = jnp.concatenate([cross_sums[:block_rows], cross_sums[block_rows:]], axis=1)
    query_wgrad, key_wgrad, value_wgrad = weight_sums
    return (
        cross_out.astype(BF16)[None],
        anchor_grad.astype(BF16)[None],
        aug_grad.astype(BF16)[None],
        query_wgrad,
        key_wgrad,
        value_wgrad,
        out_wgrad.T,
    )


def solution(mesh):
    fine = Mesh(mesh.devices.reshape(NY, 2, NZ, 2, 2), ("y", "core", "z", "xh", "xl"))
    rows = P(("y", "core"), ("z", "xh", "xl"), None)
    columns = P(None, ("z", "xh"))
    return jax.shard_map(
        body,
        mesh=fine,
        in_specs=(rows, rows, rows, columns, columns, columns, P(("z", "xh"), None)),
        out_specs=(
            rows,
            rows,
            rows,
            P(("y", "core", "xl"), ("z", "xh")),
            P(("y", "core", "xl"), ("z", "xh")),
            P(("y", "core", "xl"), ("z", "xh")),
            P(("z", "xh"), ("y", "core", "xl")),
        ),
        check_vma=False,
    )
```

```python
import functools

import jax
import jax.numpy as jnp
from jax import lax
from jax.experimental import pallas as pl
from jax.experimental.pallas import tpu as pltpu
from jax.sharding import Mesh, PartitionSpec as P

D = 4608
DB = 2304
HEADS = 32
HD = 128
NZ = 8
NY = 4
F32 = jnp.float32
BF16 = jnp.bfloat16

SOFTCAP = 50.0
EPSILON = 1e-06


def shift(block, axis, step):
    count = lax.axis_size(axis)
    return lax.ppermute(block, axis, [(i, (i + step) % count) for i in range(count)])


def swap(block, axis):
    return lax.ppermute(block, axis, [(0, 1), (1, 0)])


def times_transposed(left, right):
    return lax.dot_general(left, right, (((1,), (1,)), ((), ())), preferred_element_type=F32)


def transposed_times(left, right):
    return lax.dot_general(left, right, (((0,), (0,)), ((), ())), preferred_element_type=F32)


def added(*terms):
    total = terms[0].astype(F32)
    for term in terms[1:]:
        total = total + term.astype(F32)
    return total


def after(value, *others):
    return lax.optimization_barrier((value, *others))[0]


def rows_of(found):
    return jnp.concatenate([found[offset] for offset in range(NZ)], axis=0)


def weights_of(q, k, causal, scale):
    raw = lax.dot_general(q, k, (((1,), (1,)), ((), ())), preferred_element_type=F32) * scale
    squashed = jnp.tanh(raw * (1.0 / SOFTCAP))
    return squashed, jnp.exp(SOFTCAP * squashed) * causal


def forward_kernel(scale, q_ref, own_ref, far_ref, causal_ref, near_ref, away_ref):
    rows, width = q_ref.shape
    for head in range(width // HD):
        keys = slice(head * HD, (head + 1) * HD)
        vals = slice(width + head * HD, width + (head + 1) * HD)
        q = q_ref[:, keys]
        _, own = weights_of(q, own_ref[:, keys], causal_ref[:, :rows], scale)
        _, far = weights_of(q, far_ref[:, keys], causal_ref[:, rows:], scale)
        total = jnp.sum(own, axis=1, keepdims=True) + jnp.sum(far, axis=1, keepdims=True)
        own, far = (own / total).astype(BF16), (far / total).astype(BF16)
        att = jnp.dot(own, own_ref[:, vals], preferred_element_type=F32)
        att = att + jnp.dot(far, far_ref[:, vals], preferred_element_type=F32)
        att = att.astype(BF16)
        block = rows // (2 * NZ)
        for index in range(2 * NZ):
            to = away_ref if index % 2 else near_ref
            at = index // 2 * block
            to[at : at + block, keys] = att[index * block : (index + 1) * block]


def backward_kernel(
    scale, q_ref, own_ref, far_ref, causal_ref, near_ref, away_ref, gq_ref, mine_ref, theirs_ref
):
    rows, width = q_ref.shape
    block = rows // (2 * NZ)
    for head in range(width // HD):
        keys = slice(head * HD, (head + 1) * HD)
        vals = slice(width + head * HD, width + (head + 1) * HD)
        q = q_ref[:, keys]
        grad = jnp.concatenate(
            [
                (away_ref if index % 2 else near_ref)[
                    index // 2 * block : (index // 2 + 1) * block, keys
                ]
                for index in range(2 * NZ)
            ],
            axis=0,
        )
        squashed, probs, grads = [], [], []
        for ref, causal in ((own_ref, causal_ref[:, :rows]), (far_ref, causal_ref[:, rows:])):
            s, w = weights_of(q, ref[:, keys], causal, scale)
            squashed.append(s)
            probs.append(w)
            grads.append(
                lax.dot_general(
                    grad, ref[:, vals], (((1,), (1,)), ((), ())), preferred_element_type=F32
                )
            )
        total = sum(jnp.sum(w, axis=1, keepdims=True) for w in probs)
        probs = [w / total for w in probs]
        delta = sum(jnp.sum(g * p, axis=1, keepdims=True) for g, p in zip(grads, probs))
        gq = jnp.zeros((rows, HD), F32)
        for ref, s, p, g, to in zip(
            (own_ref, far_ref), squashed, probs, grads, (mine_ref, theirs_ref)
        ):
            scores = (p * (g - delta) * (1.0 - s * s) * scale).astype(BF16)
            gq = gq + jnp.dot(scores, ref[:, keys], preferred_element_type=F32)
            to[:, keys] = transposed_times(scores, q).astype(to.dtype)
            to[:, vals] = transposed_times(p.astype(BF16), grad).astype(to.dtype)
        gq_ref[:, keys] = gq.astype(BF16)


def kernel_call(kernel, shapes, *args):
    return pl.pallas_call(
        kernel,
        out_shape=shapes,
        in_specs=[pl.BlockSpec(memory_space=pltpu.VMEM)] * len(args),
        out_specs=[pl.BlockSpec(memory_space=pltpu.VMEM)] * len(shapes),
        compiler_params=pltpu.CompilerParams(vmem_limit_bytes=24 * 1024 * 1024),
    )(*args)


def pick(array, at, dim):
    return lax.dynamic_index_in_dim(array, at, dim, keepdims=False)


def core_split(parts):
    own_core = lax.axis_index("core")
    blocks = [part.reshape(NY, 2, 2, part.shape[0] // 16, part.shape[1]) for part in parts]
    return tuple(
        jnp.concatenate([pick(b, core, 1) for b in blocks], axis=2)
        for core in (1 - own_core, own_core)
    )


def y_split(summed):
    own_y = lax.axis_index("y")
    return tuple(pick(summed, (own_y + step) % NY, 0) for step in (0, 1, 3, 2))


def aug_split(halves):
    own_aug = lax.axis_index("xl")
    return pick(halves, own_aug, 0), pick(halves, 1 - own_aug, 0)


def split_rows(rows, parts):
    found, at = [], 0
    for part in parts:
        found.append(rows[at : at + part.shape[0] // 16])
        at += part.shape[0] // 16
    return found


def together(*values):
    return lax.optimization_barrier(values)


def body(anchor_hidden, aug_hidden, out_grad, w_query, w_key, w_value, w_out):
    score_scale = float(D // HEADS) ** (-0.5)
    block_rows = anchor_hidden.shape[1]
    row_count = block_rows * 2 * NZ
    head_width = w_query.shape[1]
    parity = lax.axis_index("xl")
    own_z, own_x = lax.axis_index("z"), lax.axis_index("xh")

    def x_pair(block):
        return jnp.concatenate([block, swap(block, "xh")], axis=0)

    def normalized(hidden):
        hidden_f = hidden.astype(F32)
        inverse = lax.rsqrt(jnp.mean(hidden_f * hidden_f, axis=1, keepdims=True) + EPSILON)
        return hidden_f * inverse, inverse

    theirs, augment = swap(anchor_hidden[0], "xh"), x_pair(aug_hidden[0])
    normal, inverse = normalized(anchor_hidden[0])
    normed = [normal.astype(BF16), normalized(theirs)[0].astype(BF16)]
    rows_in = jnp.concatenate([augment, jnp.concatenate(normed, axis=0)], axis=1)

    rings = [(rows_in, rows_in), (out_grad[0], out_grad[0])]
    found = [{0: rows_in}, {0: out_grad[0]}]

    def step(ring, number):
        rings[ring] = (shift(rings[ring][0], "z", 1), shift(rings[ring][1], "z", -1))
        found[ring][NZ - number], found[ring][number] = rings[ring]

    def last_step(ring, cut):
        behind, ahead = rings[ring]
        half = behind.shape[cut] // 2
        low = lax.slice_in_dim(behind, 0, half, axis=cut)
        high = lax.slice_in_dim(ahead, half, 2 * half, axis=cut)
        halves = [shift(low, "z", 1), shift(high, "z", -1)]
        found[ring][NZ // 2] = jnp.concatenate(halves, axis=cut)

    step(1, 1)
    step(0, 1)
    step(1, 2)
    cot_sent = jnp.concatenate([found[1][offset] for offset in (6, 7, 0, 1, 2)], axis=0)
    rings[1], rings[0], cot_sent = together(rings[1], rings[0], cot_sent)
    cot_first = swap(cot_sent, "xh")
    step(0, 2)
    step(1, 3)
    last_step(1, 1)
    cot_sent = jnp.concatenate([found[1][offset] for offset in (3, 4, 5)], axis=0)
    rings[0], cot_sent = together(rings[0], cot_sent)
    step(0, 3)
    rings[0], cot_first = together(rings[0], cot_first)
    cot_second = swap(cot_sent, "xh")
    last_step(0, 0)
    rows_in, cot_near = rows_of(found[0]), rows_of(found[1])
    cot_away = jnp.concatenate(
        [cot_first[2 * block_rows :], cot_second, cot_first[: 2 * block_rows]], axis=0
    )
    augment_all, normed_all = rows_in[:, :DB], rows_in[:, DB:]

    counter = jnp.arange(row_count, dtype=jnp.int32)
    shard_z = (counter // (2 * block_rows) + own_z) % NZ
    half = (counter // block_rows + own_x) % 2
    shard = (shard_z * 2 + half) * 2
    own_place = (shard + parity) * block_rows + counter % block_rows
    far_place = (shard + 1 - parity) * block_rows + counter % block_rows
    key_place = jnp.concatenate([own_place, far_place], axis=0)
    causal = (key_place[None, :] <= own_place[:, None]).astype(F32)

    keys_own = jnp.dot(augment_all, w_key, preferred_element_type=F32).astype(BF16)
    values_own = jnp.dot(augment_all, w_value, preferred_element_type=F32).astype(BF16)
    both_own = jnp.concatenate([keys_own, values_own], axis=1)
    both_far = swap(both_own, "xl")
    query = jnp.dot(normed_all, w_query, preferred_element_type=F32).astype(BF16)

    square = jax.ShapeDtypeStruct((row_count, head_width), BF16)
    wide = (row_count, 2 * head_width)
    halfway = jax.ShapeDtypeStruct((row_count // 2, head_width), BF16)
    near, away = kernel_call(
        functools.partial(forward_kernel, score_scale),
        [halfway, halfway],
        query,
        both_own,
        both_far,
        causal,
    )
    def cross_of(rows):
        sides = [w_out[:, :DB], w_out[:, DB:]]
        return jnp.stack(
            [jnp.dot(rows, side, preferred_element_type=F32).astype(BF16) for side in sides]
        )

    def cross_block(array, offset):
        return array[:, offset % NZ * block_rows :][:, :block_rows]

    def cross_sent(*offsets):
        return jnp.concatenate([cross_block(cross_away, offset) for offset in offsets], axis=1)

    cross_away = cross_of(away)
    back = {(4,): cross_block(cross_away, 4)}
    grad_near = times_transposed(cot_near, w_out).astype(BF16)
    grad_away = times_transposed(cot_away, w_out).astype(BF16)
    grad_query, mine, theirs = kernel_call(
        functools.partial(backward_kernel, score_scale),
        [square, jax.ShapeDtypeStruct(wide, F32), jax.ShapeDtypeStruct(wide, BF16)],
        query,
        both_own,
        both_far,
        causal,
        grad_near,
        grad_away,
    )

    theirs, grad_query, mine, near, away, back, cross_away = together(
        theirs, grad_query, mine, near, away, back, cross_away
    )
    theirs = swap(theirs, "xl")
    back[4,] = swap(back[4,], "xh")
    cross_own = cross_of(near)
    normed_terms = [
        times_transposed(grad_query, w_query[:DB]).astype(BF16),
        times_transposed(grad_query, w_query[DB:]).astype(BF16),
    ]
    for offsets in ((3, -3), (2, -2), (1, -1, 0)):
        back[offsets] = cross_sent(*offsets)
    theirs, back, cross_own, normed_terms, near, away = together(
        theirs, back, cross_own, normed_terms, near, away
    )
    grad_both = added(mine, theirs).astype(BF16)
    grad_keys, grad_values = grad_both[:, :head_width], grad_both[:, head_width:]
    aug_terms = times_transposed(grad_keys, w_key) + times_transposed(grad_values, w_value)
    ring_terms = jnp.stack([aug_terms.astype(BF16), *normed_terms])

    def chunks(*offsets):
        found = []
        for offset in offsets:
            at = offset % NZ * 2 * block_rows
            sent = next(sent for sent in back if offset in sent)
            received = back[sent][:, sent.index(offset) * block_rows :][:, :block_rows]
            cross = added(cross_block(cross_own, offset), received).astype(BF16)
            cross = cross.reshape(1, 2 * block_rows, DB)
            found.append(jnp.concatenate([ring_terms[:, at : at + 2 * block_rows], cross], axis=0))
        return found

    (far,) = chunks(4)
    ahead, behind = far[:, :block_rows], far[:, block_rows:]
    ahead, behind, back, grad_both, near, away = together(
        ahead, behind, back, grad_both, near, away
    )
    ahead, behind = shift(ahead, "z", 1), shift(behind, "z", -1)
    back[3, -3] = swap(back[3, -3], "xh")
    early_parts = [
        (transposed_times(cot_near, near) + transposed_times(cot_away, away)).astype(BF16)
    ]
    early_send, early_keep = core_split(early_parts)
    early = list(y_split(added(early_keep, swap(early_send, "core")).astype(BF16)))
    both_part = transposed_times(augment_all, grad_both).astype(BF16)
    late_parts = [
        transposed_times(normed_all, grad_query).astype(BF16),
        both_part[:, :head_width],
        both_part[:, head_width:],
    ]
    late_send, late_keep = core_split(late_parts)
    late_back = swap(late_send, "core")
    up, down = chunks(3, -3)
    up, down = ((part[:, :block_rows], part[:, block_rows:]) for part in (up, down))

    ahead, behind, up, down, back, late_keep, late_back, early = together(
        ahead, behind, up, down, back, late_keep, late_back, early
    )
    ahead = jnp.concatenate([added(up[0], ahead).astype(BF16), up[1]], axis=1)
    behind = jnp.concatenate([down[0], added(down[1], behind).astype(BF16)], axis=1)
    ahead, behind, back, late_keep, late_back, early = together(
        ahead, behind, back, late_keep, late_back, early
    )
    ahead, behind = shift(ahead, "z", 1), shift(behind, "z", -1)
    back[2, -2] = swap(back[2, -2], "xh")
    early[1], early[2] = shift(early[1], "y", 1), shift(early[2], "y", 3)
    early[3] = shift(after(early[3], early[1]), "y", 2)
    late = list(y_split(added(late_keep, late_back).astype(BF16)))
    up, down = chunks(2, -2)

    ahead, behind, up, down, back, early, late = together(
        ahead, behind, up, down, back, early, late
    )
    ahead, behind = added(up, ahead).astype(BF16), added(down, behind).astype(BF16)
    ahead, behind, back, early, late = together(ahead, behind, back, early, late)
    ahead, behind = shift(ahead, "z", 1), shift(behind, "z", -1)
    back[1, -1, 0] = swap(back[1, -1, 0], "xh")
    late[1], late[2] = shift(late[1], "y", 1), shift(late[2], "y", 3)
    early_keep, early_send = aug_split(added(*early).astype(BF16))
    up, down, near = chunks(1, -1, 0)

    ahead, behind, up, down, near, early_keep, early_send, late = together(
        ahead, behind, up, down, near, early_keep, early_send, late
    )
    ahead, behind = added(up, ahead).astype(BF16), added(down, behind).astype(BF16)
    ahead, behind, near, early_send, late = together(ahead, behind, near, early_send, late)
    ahead, behind = shift(ahead, "z", 1), shift(behind, "z", -1)
    late[3] = shift(late[3], "y", 2)
    out_wgrad = added(early_keep, swap(early_send, "xl"))

    ahead, behind, out_wgrad = together(ahead, behind, out_wgrad)
    theirs = added(*(part[:3, block_rows:] for part in (near, ahead, behind))).astype(BF16)
    late_keep, late_send = aug_split(added(*late).astype(BF16))
    theirs, late_send = swap(theirs, "xh"), swap(late_send, "xl")
    weight_sums = [
        added(keep, sent)
        for keep, sent in zip(split_rows(late_keep, late_parts), split_rows(late_send, late_parts))
    ]
    row_sums = added(*(part[:3, :block_rows] for part in (near, ahead, behind)))
    theirs, weight_sums, row_sums = together(theirs, weight_sums, row_sums)
    aug_grad = added(row_sums[0], theirs[0])
    grad_normed = [added(row_sums[side], theirs[side]) for side in (1, 2)]
    cross_sums = added(near[3], ahead[3], behind[3])

    grad_normed = jnp.concatenate(grad_normed, axis=1)
    inner = jnp.mean(grad_normed * normal, axis=1, keepdims=True)
    anchor_grad = inverse * (grad_normed - normal * inner)
    cross_out = jnp.concatenate([cross_sums[:block_rows], cross_sums[block_rows:]], axis=1)
    query_wgrad, key_wgrad, value_wgrad = weight_sums
    return (
        cross_out.astype(BF16)[None],
        anchor_grad.astype(BF16)[None],
        aug_grad.astype(BF16)[None],
        query_wgrad,
        key_wgrad,
        value_wgrad,
        out_wgrad.T,
    )


def solution(mesh):
    fine = Mesh(mesh.devices.reshape(NY, 2, NZ, 2, 2), ("y", "core", "z", "xh", "xl"))
    rows = P(("y", "core"), ("z", "xh", "xl"), None)
    columns = P(None, ("z", "xh"))
    return jax.shard_map(
        body,
        mesh=fine,
        in_specs=(rows, rows, rows, columns, columns, columns, P(("z", "xh"), None)),
        out_specs=(
            rows,
            rows,
            rows,
            P(("y", "core", "xl"), ("z", "xh")),
            P(("y", "core", "xl"), ("z", "xh")),
            P(("y", "core", "xl"), ("z", "xh")),
            P(("z", "xh"), ("y", "core", "xl")),
        ),
        check_vma=False,
    )
```

```python
import functools

import jax
import jax.numpy as jnp
from jax import lax
from jax.experimental import pallas as pl
from jax.experimental.pallas import tpu as pltpu
from jax.sharding import Mesh, PartitionSpec as P

D = 4608
DB = 2304
HEADS = 32
HD = 128
NZ = 8
NY = 4
F32 = jnp.float32
BF16 = jnp.bfloat16

SOFTCAP = 50.0
EPSILON = 1e-06


def shift(block, axis, step):
    count = lax.axis_size(axis)
    return lax.ppermute(block, axis, [(i, (i + step) % count) for i in range(count)])


def swap(block, axis):
    return lax.ppermute(block, axis, [(0, 1), (1, 0)])


def times_transposed(left, right):
    return lax.dot_general(left, right, (((1,), (1,)), ((), ())), preferred_element_type=F32)


def transposed_times(left, right):
    return lax.dot_general(left, right, (((0,), (0,)), ((), ())), preferred_element_type=F32)


def added(*terms):
    total = terms[0].astype(F32)
    for term in terms[1:]:
        total = total + term.astype(F32)
    return total


def after(value, *others):
    return lax.optimization_barrier((value, *others))[0]


def rows_of(found):
    return jnp.concatenate([found[offset] for offset in range(NZ)], axis=0)


def weights_of(q, k, causal, scale):
    raw = lax.dot_general(q, k, (((1,), (1,)), ((), ())), preferred_element_type=F32) * scale
    squashed = jnp.tanh(raw * (1.0 / SOFTCAP))
    return squashed, jnp.exp(SOFTCAP * squashed) * causal


def forward_kernel(scale, q_ref, own_ref, far_ref, causal_ref, near_ref, away_ref):
    rows, width = q_ref.shape
    for head in range(width // HD):
        keys = slice(head * HD, (head + 1) * HD)
        vals = slice(width + head * HD, width + (head + 1) * HD)
        q = q_ref[:, keys]
        _, own = weights_of(q, own_ref[:, keys], causal_ref[:, :rows], scale)
        _, far = weights_of(q, far_ref[:, keys], causal_ref[:, rows:], scale)
        total = jnp.sum(own, axis=1, keepdims=True) + jnp.sum(far, axis=1, keepdims=True)
        own, far = (own / total).astype(BF16), (far / total).astype(BF16)
        att = jnp.dot(own, own_ref[:, vals], preferred_element_type=F32)
        att = att + jnp.dot(far, far_ref[:, vals], preferred_element_type=F32)
        att = att.astype(BF16)
        block = rows // (2 * NZ)
        for index in range(2 * NZ):
            to = away_ref if index % 2 else near_ref
            at = index // 2 * block
            to[at : at + block, keys] = att[index * block : (index + 1) * block]


def backward_kernel(
    scale, q_ref, own_ref, far_ref, causal_ref, near_ref, away_ref, gq_ref, mine_ref, theirs_ref
):
    rows, width = q_ref.shape
    block = rows // (2 * NZ)
    for head in range(width // HD):
        keys = slice(head * HD, (head + 1) * HD)
        vals = slice(width + head * HD, width + (head + 1) * HD)
        q = q_ref[:, keys]
        grad = jnp.concatenate(
            [
                (away_ref if index % 2 else near_ref)[
                    index // 2 * block : (index // 2 + 1) * block, keys
                ]
                for index in range(2 * NZ)
            ],
            axis=0,
        )
        squashed, probs, grads = [], [], []
        for ref, causal in ((own_ref, causal_ref[:, :rows]), (far_ref, causal_ref[:, rows:])):
            s, w = weights_of(q, ref[:, keys], causal, scale)
            squashed.append(s)
            probs.append(w)
            grads.append(
                lax.dot_general(
                    grad, ref[:, vals], (((1,), (1,)), ((), ())), preferred_element_type=F32
                )
            )
        total = sum(jnp.sum(w, axis=1, keepdims=True) for w in probs)
        probs = [w / total for w in probs]
        delta = sum(jnp.sum(g * p, axis=1, keepdims=True) for g, p in zip(grads, probs))
        gq = jnp.zeros((rows, HD), F32)
        for ref, s, p, g, to in zip(
            (own_ref, far_ref), squashed, probs, grads, (mine_ref, theirs_ref)
        ):
            scores = (p * (g - delta) * (1.0 - s * s) * scale).astype(BF16)
            gq = gq + jnp.dot(scores, ref[:, keys], preferred_element_type=F32)
            to[:, keys] = transposed_times(scores, q).astype(to.dtype)
            to[:, vals] = transposed_times(p.astype(BF16), grad).astype(to.dtype)
        gq_ref[:, keys] = gq.astype(BF16)


def kernel_call(kernel, shapes, *args):
    return pl.pallas_call(
        kernel,
        out_shape=shapes,
        in_specs=[pl.BlockSpec(memory_space=pltpu.VMEM)] * len(args),
        out_specs=[pl.BlockSpec(memory_space=pltpu.VMEM)] * len(shapes),
        compiler_params=pltpu.CompilerParams(vmem_limit_bytes=24 * 1024 * 1024),
    )(*args)


def pick(array, at, dim):
    return lax.dynamic_index_in_dim(array, at, dim, keepdims=False)


def core_split(parts):
    own_core = lax.axis_index("core")
    blocks = [part.reshape(NY, 2, 2, part.shape[0] // 16, part.shape[1]) for part in parts]
    return tuple(
        jnp.concatenate([pick(b, core, 1) for b in blocks], axis=2)
        for core in (1 - own_core, own_core)
    )


def y_split(summed):
    own_y = lax.axis_index("y")
    return tuple(pick(summed, (own_y + step) % NY, 0) for step in (0, 1, 3, 2))


def aug_split(halves):
    own_aug = lax.axis_index("xl")
    return pick(halves, own_aug, 0), pick(halves, 1 - own_aug, 0)


def split_rows(rows, parts):
    found, at = [], 0
    for part in parts:
        found.append(rows[at : at + part.shape[0] // 16])
        at += part.shape[0] // 16
    return found


def together(*values):
    return lax.optimization_barrier(values)


def body(anchor_hidden, aug_hidden, out_grad, w_query, w_key, w_value, w_out):
    score_scale = float(D // HEADS) ** (-0.5)
    block_rows = anchor_hidden.shape[1]
    row_count = block_rows * 2 * NZ
    head_width = w_query.shape[1]
    parity = lax.axis_index("xl")
    own_z, own_x = lax.axis_index("z"), lax.axis_index("xh")

    def x_pair(block):
        return jnp.concatenate([block, swap(block, "xh")], axis=0)

    def normalized(hidden):
        hidden_f = hidden.astype(F32)
        inverse = lax.rsqrt(jnp.mean(hidden_f * hidden_f, axis=1, keepdims=True) + EPSILON)
        return hidden_f * inverse, inverse

    theirs, augment = swap(anchor_hidden[0], "xh"), x_pair(aug_hidden[0])
    normal, inverse = normalized(anchor_hidden[0])
    normed = [normal.astype(BF16), normalized(theirs)[0].astype(BF16)]
    rows_in = jnp.concatenate([augment, jnp.concatenate(normed, axis=0)], axis=1)

    rings = [(rows_in, rows_in), (out_grad[0], out_grad[0])]
    found = [{0: rows_in}, {0: out_grad[0]}]

    def step(ring, number):
        rings[ring] = (shift(rings[ring][0], "z", 1), shift(rings[ring][1], "z", -1))
        found[ring][NZ - number], found[ring][number] = rings[ring]

    def last_step(ring, cut):
        behind, ahead = rings[ring]
        half = behind.shape[cut] // 2
        low = lax.slice_in_dim(behind, 0, half, axis=cut)
        high = lax.slice_in_dim(ahead, half, 2 * half, axis=cut)
        halves = [shift(low, "z", 1), shift(high, "z", -1)]
        found[ring][NZ // 2] = jnp.concatenate(halves, axis=cut)

    step(1, 1)
    step(0, 1)
    step(1, 2)
    cot_sent = jnp.concatenate([found[1][offset] for offset in (6, 7, 0, 1, 2)], axis=0)
    rings[1], rings[0], cot_sent = together(rings[1], rings[0], cot_sent)
    cot_first = swap(cot_sent, "xh")
    step(0, 2)
    step(1, 3)
    last_step(1, 1)
    cot_sent = jnp.concatenate([found[1][offset] for offset in (3, 4, 5)], axis=0)
    rings[0], cot_sent = together(rings[0], cot_sent)
    step(0, 3)
    w_both = jnp.concatenate([w_key, w_value], axis=1)
    rings[0], cot_first, w_both = together(rings[0], cot_first, w_both)
    cot_second = swap(cot_sent, "xh")
    last_step(0, 0)
    rows_in, cot_near = rows_of(found[0]), rows_of(found[1])
    cot_away = jnp.concatenate(
        [cot_first[2 * block_rows :], cot_second, cot_first[: 2 * block_rows]], axis=0
    )
    augment_all, normed_all = rows_in[:, :DB], rows_in[:, DB:]

    counter = jnp.arange(row_count, dtype=jnp.int32)
    shard_z = (counter // (2 * block_rows) + own_z) % NZ
    half = (counter // block_rows + own_x) % 2
    shard = (shard_z * 2 + half) * 2
    own_place = (shard + parity) * block_rows + counter % block_rows
    far_place = (shard + 1 - parity) * block_rows + counter % block_rows
    key_place = jnp.concatenate([own_place, far_place], axis=0)
    causal = (key_place[None, :] <= own_place[:, None]).astype(F32)

    both_own = jnp.dot(augment_all, w_both, preferred_element_type=F32).astype(BF16)
    both_far = swap(both_own, "xl")
    query = jnp.dot(normed_all, w_query, preferred_element_type=F32).astype(BF16)

    square = jax.ShapeDtypeStruct((row_count, head_width), BF16)
    wide = (row_count, 2 * head_width)
    halfway = jax.ShapeDtypeStruct((row_count // 2, head_width), BF16)
    near, away = kernel_call(
        functools.partial(forward_kernel, score_scale),
        [halfway, halfway],
        query,
        both_own,
        both_far,
        causal,
    )
    def cross_of(rows):
        sides = [w_out[:, :DB], w_out[:, DB:]]
        return jnp.stack(
            [jnp.dot(rows, side, preferred_element_type=F32).astype(BF16) for side in sides]
        )

    def cross_block(array, offset):
        return array[:, offset % NZ * block_rows :][:, :block_rows]

    def cross_sent(*offsets):
        return jnp.concatenate([cross_block(cross_away, offset) for offset in offsets], axis=1)

    cross_away = cross_of(away)
    back = {(4,): cross_block(cross_away, 4)}
    grad_near = times_transposed(cot_near, w_out).astype(BF16)
    grad_away = times_transposed(cot_away, w_out).astype(BF16)
    grad_query, mine, theirs = kernel_call(
        functools.partial(backward_kernel, score_scale),
        [square, jax.ShapeDtypeStruct(wide, F32), jax.ShapeDtypeStruct(wide, BF16)],
        query,
        both_own,
        both_far,
        causal,
        grad_near,
        grad_away,
    )

    theirs, grad_query, mine, near, away, back, cross_away = together(
        theirs, grad_query, mine, near, away, back, cross_away
    )
    theirs = swap(theirs, "xl")
    back[4,] = swap(back[4,], "xh")
    cross_own = cross_of(near)
    normed_terms = [
        times_transposed(grad_query, w_query[:DB]).astype(BF16),
        times_transposed(grad_query, w_query[DB:]).astype(BF16),
    ]
    for offsets in ((3, -3), (2, -2), (1, -1, 0)):
        back[offsets] = cross_sent(*offsets)
    theirs, back, cross_own, normed_terms, near, away = together(
        theirs, back, cross_own, normed_terms, near, away
    )
    grad_both = added(mine, theirs).astype(BF16)
    grad_keys, grad_values = grad_both[:, :head_width], grad_both[:, head_width:]
    aug_terms = times_transposed(grad_keys, w_key) + times_transposed(grad_values, w_value)
    ring_terms = jnp.stack([aug_terms.astype(BF16), *normed_terms])

    def chunks(*offsets):
        found = []
        for offset in offsets:
            at = offset % NZ * 2 * block_rows
            sent = next(sent for sent in back if offset in sent)
            received = back[sent][:, sent.index(offset) * block_rows :][:, :block_rows]
            cross = added(cross_block(cross_own, offset), received).astype(BF16)
            cross = cross.reshape(1, 2 * block_rows, DB)
            found.append(jnp.concatenate([ring_terms[:, at : at + 2 * block_rows], cross], axis=0))
        return found

    (far,) = chunks(4)
    ahead, behind = far[:, :block_rows], far[:, block_rows:]
    ahead, behind, back, grad_both, near, away = together(
        ahead, behind, back, grad_both, near, away
    )
    ahead, behind = shift(ahead, "z", 1), shift(behind, "z", -1)
    back[3, -3] = swap(back[3, -3], "xh")
    early_parts = [
        (transposed_times(cot_near, near) + transposed_times(cot_away, away)).astype(BF16)
    ]
    early_send, early_keep = core_split(early_parts)
    early = list(y_split(added(early_keep, swap(early_send, "core")).astype(BF16)))
    both_part = transposed_times(augment_all, grad_both).astype(BF16)
    late_parts = [
        transposed_times(normed_all, grad_query).astype(BF16),
        both_part[:, :head_width],
        both_part[:, head_width:],
    ]
    late_send, late_keep = core_split(late_parts)
    late_back = swap(late_send, "core")
    up, down = chunks(3, -3)
    up, down = ((part[:, :block_rows], part[:, block_rows:]) for part in (up, down))

    ahead, behind, up, down, back, late_keep, late_back, early = together(
        ahead, behind, up, down, back, late_keep, late_back, early
    )
    ahead = jnp.concatenate([added(up[0], ahead).astype(BF16), up[1]], axis=1)
    behind = jnp.concatenate([down[0], added(down[1], behind).astype(BF16)], axis=1)
    ahead, behind, back, late_keep, late_back, early = together(
        ahead, behind, back, late_keep, late_back, early
    )
    ahead, behind = shift(ahead, "z", 1), shift(behind, "z", -1)
    back[2, -2] = swap(back[2, -2], "xh")
    early[1], early[2] = shift(early[1], "y", 1), shift(early[2], "y", 3)
    early[3] = shift(after(early[3], early[1]), "y", 2)
    late = list(y_split(added(late_keep, late_back).astype(BF16)))
    up, down = chunks(2, -2)

    ahead, behind, up, down, back, early, late = together(
        ahead, behind, up, down, back, early, late
    )
    ahead, behind = added(up, ahead).astype(BF16), added(down, behind).astype(BF16)
    ahead, behind, back, early, late = together(ahead, behind, back, early, late)
    ahead, behind = shift(ahead, "z", 1), shift(behind, "z", -1)
    back[1, -1, 0] = swap(back[1, -1, 0], "xh")
    late[1], late[2] = shift(late[1], "y", 1), shift(late[2], "y", 3)
    early_keep, early_send = aug_split(added(*early).astype(BF16))
    up, down, near = chunks(1, -1, 0)

    ahead, behind, up, down, near, early_keep, early_send, late = together(
        ahead, behind, up, down, near, early_keep, early_send, late
    )
    ahead, behind = added(up, ahead).astype(BF16), added(down, behind).astype(BF16)
    ahead, behind, near, early_send, late = together(ahead, behind, near, early_send, late)
    ahead, behind = shift(ahead, "z", 1), shift(behind, "z", -1)
    late[3] = shift(late[3], "y", 2)
    out_wgrad = added(early_keep, swap(early_send, "xl"))

    ahead, behind, out_wgrad = together(ahead, behind, out_wgrad)
    theirs = added(*(part[:3, block_rows:] for part in (near, ahead, behind))).astype(BF16)
    late_keep, late_send = aug_split(added(*late).astype(BF16))
    theirs, late_send = swap(theirs, "xh"), swap(late_send, "xl")
    weight_sums = [
        added(keep, sent)
        for keep, sent in zip(split_rows(late_keep, late_parts), split_rows(late_send, late_parts))
    ]
    row_sums = added(*(part[:3, :block_rows] for part in (near, ahead, behind)))
    theirs, weight_sums, row_sums = together(theirs, weight_sums, row_sums)
    aug_grad = added(row_sums[0], theirs[0])
    grad_normed = [added(row_sums[side], theirs[side]) for side in (1, 2)]
    cross_sums = added(near[3], ahead[3], behind[3])

    grad_normed = jnp.concatenate(grad_normed, axis=1)
    inner = jnp.mean(grad_normed * normal, axis=1, keepdims=True)
    anchor_grad = inverse * (grad_normed - normal * inner)
    cross_out = jnp.concatenate([cross_sums[:block_rows], cross_sums[block_rows:]], axis=1)
    query_wgrad, key_wgrad, value_wgrad = weight_sums
    return (
        cross_out.astype(BF16)[None],
        anchor_grad.astype(BF16)[None],
        aug_grad.astype(BF16)[None],
        query_wgrad,
        key_wgrad,
        value_wgrad,
        out_wgrad.T,
    )


def solution(mesh):
    fine = Mesh(mesh.devices.reshape(NY, 2, NZ, 2, 2), ("y", "core", "z", "xh", "xl"))
    rows = P(("y", "core"), ("z", "xh", "xl"), None)
    columns = P(None, ("z", "xh"))
    return jax.shard_map(
        body,
        mesh=fine,
        in_specs=(rows, rows, rows, columns, columns, columns, P(("z", "xh"), None)),
        out_specs=(
            rows,
            rows,
            rows,
            P(("y", "core", "xl"), ("z", "xh")),
            P(("y", "core", "xl"), ("z", "xh")),
            P(("y", "core", "xl"), ("z", "xh")),
            P(("z", "xh"), ("y", "core", "xl")),
        ),
        check_vma=False,
    )
```
